256 devices in a mesh: cuts: 8 (over x, y_hi), fsdp: 32 (over z, y_lo, core).
Axes of the slice: x: 4, y: 4 (y_hi: 2, y_lo: 2; y = y_hi * 2 + y_lo), z: 8, core: 2. Of those that a mesh axis runs over, the one named last changes fastest.
Arguments:
- local_params: bfloat16 [8, 32, 128, 8192], P('cuts', 'fsdp'), may hold values from -6 to 6
- outer_params: bfloat16 [32, 128, 8192], P('fsdp'), may hold values from -6 to 6
- column_signs: int32 [8192], replicated, may hold values from 0 to 1
- delta_exponents: int32 [8, 32, 128, 64], P('cuts', 'fsdp'), may hold values from -8 to -6
- outer_master: float32 [32, 128, 8192], P(None, 'cuts', 'fsdp'), may hold values from -6 to 6
- outer_momentum: float32 [32, 128, 8192], P(None, 'cuts', 'fsdp'), may hold values from -3 to 3
- master_exponents: int32 [32, 128, 64], P(None, 'cuts', 'fsdp'), may hold values from -8 to -6
Outputs:
- outer_new: bfloat16 [32, 128, 8192], P('fsdp')
- master_new: float32 [32, 128, 8192], P(None, 'cuts', 'fsdp')
- momentum_new: float32 [32, 128, 8192], P(None, 'cuts', 'fsdp')
The draws below stay inside these ranges and needn't reach their ends.
All inputs are finite; a program needn't handle non-finite values.
Results may differ from the reference program's by a relative error of at most 0.013.
Values may be sent and summed in bfloat16 or wider, within the bound.
A program may use at most 64 MiB of HBM per device.

```python
import math
import jax
import jax.numpy as jnp
from jax import lax

D = 8192
HB = 128
RS = 128
SHARDS = 32
REPLICAS = 8
SCALES = 64


def touch_ends(values, stream_key, low, high):
    dims = values.shape
    index_at = [jax.random.randint(jax.random.fold_in(stream_key, axis), (), 0, dims[axis]) for axis in range(len(dims))]
    values = values.at[tuple(index_at)].set(low)
    longest = dims.index(max(dims))
    index_at[longest] = (index_at[longest] + 1) % dims[longest]
    return values.at[tuple(index_at)].set(high)


def level_of(own_key, extent, pieces, least, top_value):
    factor_of, own = 1.0, jax.random.fold_in(own_key, 6)
    for dim, shards_of in pieces:
        heights = jnp.exp(jax.random.uniform(jax.random.fold_in(own, dim), (shards_of,), jnp.float32, least / len(pieces), top_value / len(pieces)))
        factor_of = factor_of * jnp.repeat(heights, extent[dim] // shards_of).reshape([-1 if axis == dim else 1 for axis in range(len(extent))])
    return factor_of


def noise(key, shape, spread, bound, shards=(), kind=jnp.bfloat16):
    gain = level_of(key, shape, shards, -0.22, 0.18) if shards else 1.0
    values = jax.random.normal(key, shape, jnp.float32) * spread * gain
    return jnp.minimum(jnp.maximum(values, -bound), bound).astype(kind)


def setup_inputs(seed: int = 0) -> dict:
    keys = jax.random.split(jax.random.key(seed), 8)
    local_params = noise(keys[0], (REPLICAS, SHARDS, RS, D), 1.0, 6.0, ((0, 8), (1, 32)))
    outer_params = noise(keys[1], (SHARDS, RS, D), 1.0, 6.0, ((0, 32),))
    column_signs = touch_ends(jax.random.randint(keys[2], (D,), 0, 2), jax.random.fold_in(keys[2], 1), 0, 1).astype(jnp.int32)
    delta_exponents = touch_ends(jax.random.randint(keys[3], (REPLICAS, SHARDS, RS, SCALES), -8, -5), jax.random.fold_in(keys[3], 1), -8, (-5) - 1).astype(jnp.int32)
    outer_master = noise(keys[4], (SHARDS, RS, D), 1.0, 6.0, ((1, 8), (2, 32)), jnp.float32)
    outer_momentum = noise(keys[5], (SHARDS, RS, D), 0.5, 3.0, ((1, 8), (2, 32)), jnp.float32)
    master_exponents = touch_ends(jax.random.randint(keys[6], (SHARDS, RS, SCALES), -8, -5), jax.random.fold_in(keys[6], 1), -8, (-5) - 1).astype(jnp.int32)
    return {"local_params": local_params, "outer_params": outer_params, "column_signs": column_signs, "delta_exponents": delta_exponents, "outer_master": outer_master, "outer_momentum": outer_momentum, "master_exponents": master_exponents}


CLIP_LIMIT = 448.0
OUTER_RATE = 0.7
MOMENTUM_DECAY = 0.9

def hadamard_table(order):
    index = jnp.arange(order, dtype=jnp.int32)
    parity = jnp.zeros((order, order), jnp.int32)
    for bit_number in range(order.bit_length() - 1):
        row_bits = jnp.bitwise_and(jnp.right_shift(index, bit_number), 1)
        parity = parity + row_bits[:, None] * row_bits[None, :]
    signed = 1 - 2 * jnp.bitwise_and(parity, 1)
    return signed.astype(jnp.float32) * (1.0 / math.sqrt(order))

def rotate_blocks(values, table):
    shaped = values.reshape(values.shape[:-1] + (values.shape[-1] // HB, HB))
    turned = jnp.einsum('...k,kj->...j', shaped, table, precision=lax.Precision.HIGHEST)
    return turned.reshape(values.shape)

def block_scale(values, exponents):
    shaped = values.reshape(values.shape[:-1] + (exponents.shape[-1], HB))
    factor = jnp.exp2(exponents.astype(jnp.float32))
    return (shaped * factor[..., None]).reshape(values.shape)

def encode(values, flips, exponents, table):
    rotated = rotate_blocks(values * flips, table)
    scaled = block_scale(rotated, -exponents)
    return jnp.clip(scaled, -CLIP_LIMIT, CLIP_LIMIT).astype(jnp.bfloat16)

def decode_rotated(encoded, exponents):
    return block_scale(encoded.astype(jnp.float32), exponents)

def unrotate(values, flips, table):
    return rotate_blocks(values, table) * flips

def reference(local_params, outer_params, column_signs, delta_exponents, outer_master, outer_momentum, master_exponents):
    table = hadamard_table(HB)
    flips = (1 - 2 * column_signs).astype(jnp.float32)

    def one_shard(shard):
        outer_rows = outer_params[shard].astype(jnp.float32)
        local_rows = local_params[:, shard].astype(jnp.float32)
        delta = outer_rows[None] - local_rows
        exps_rows = delta_exponents[:, shard]
        encoded = encode(delta, flips, exps_rows, table)
        return lax.optimization_barrier(jnp.sum(decode_rotated(encoded, exps_rows), axis=0))
    summed = lax.map(one_shard, jnp.arange(SHARDS, dtype=jnp.int32))
    gradient = unrotate(summed / REPLICAS, flips, table)
    momentum_new = MOMENTUM_DECAY * outer_momentum + gradient
    master_new = outer_master - OUTER_RATE * (gradient + MOMENTUM_DECAY * momentum_new)
    encoded_new = encode(master_new, flips, master_exponents, table)
    outer_new = unrotate(decode_rotated(encoded_new, master_exponents), flips, table).astype(jnp.bfloat16)
    return (outer_new, master_new, momentum_new)
```

```python
import functools
import math

import jax
import jax.numpy as jnp
from jax import lax
from jax.experimental import pallas as pl
from jax.experimental.pallas import tpu as pltpu
from jax.sharding import PartitionSpec as P

HB = 128
RB = 16
OW = 256
CUTS = 8
FSDP = 32
DIM = FSDP * OW
ROWS = CUTS * RB
LIMIT = 448.0 * math.sqrt(HB)
OUTER_RATE = 0.7
DECAY = 0.9
KEEP_MOMENTUM = OUTER_RATE * DECAY * DECAY
GRAD_IN_MASTER = OUTER_RATE * (1.0 + DECAY)
MESH = pl.DeviceIdType.MESH

XA, XB, YH = 0, 1, 2
ORDERS = ((XA, XB, YH), (XB, YH, XA), (YH, XA, XB))
SIZES = (6, 5, 5, 5, 6, 5)


def column_groups():
    groups, start = [], 0
    for k, n in enumerate(SIZES):
        groups.append((start, n, ORDERS[k % 3]))
        start += n
    assert start == FSDP
    return groups


GROUPS = column_groups()
NG = len(GROUPS)


def sylvester(order):
    i = lax.broadcasted_iota(jnp.int32, (order, order), 0)
    j = lax.broadcasted_iota(jnp.int32, (order, order), 1)
    t = jnp.bitwise_and(i, j)
    for s in (4, 2, 1):
        t = jnp.bitwise_xor(t, jnp.right_shift(t, s))
    return (1 - 2 * jnp.bitwise_and(t, 1)).astype(jnp.float32)


def power(exponents):
    return jnp.exp2(exponents.astype(jnp.float32)).astype(jnp.bfloat16)


def kernel(
    local_hbm, outer_hbm, signs_hbm, dexp_hbm, master_hbm, mom_hbm, mexp_hbm,
    out_hbm, master_out, mom_out,
    lv, ov, sv, so, dexp_v, thr, master_v, mom_v, mexp_v, master_o, mom_o,
    w1, bd, asrc, abuf, sbuf, srecv,
    *rest,
):
    parts, r1, r2, r3, res = (rest[k * NG:(k + 1) * NG] for k in range(5))
    (ld_sem, in_sem, rs_send, rs_recv, ag_send, ag_recv, a1_sem, a2_sem, out_sem) = rest[5 * NG:]
    c, f = lax.axis_index("cuts"), lax.axis_index("fsdp")
    x, yh = lax.div(c, 2), lax.rem(c, 2)
    v = lax.div(x, 2)
    u = lax.rem(lax.rem(x, 2) + v, 2)
    flip_x = x + 1 - 2 * lax.rem(x, 2)
    partner = (
        (flip_x * 2 + yh, f),
        ((3 - x) * 2 + yh, f),
        (x * 2 + 1 - yh, f),
    )

    def first_row(order, bits):
        mine = [u, v, yh]
        for d, b in zip(order, bits):
            mine[d] = lax.rem(mine[d] + b, 2)
        au, av, ay = mine
        ax = av * 2 + lax.rem(au + av, 2)
        return pl.multiple_of((ax * 2 + ay) * RB, RB)

    barrier = pltpu.get_barrier_semaphore()
    for p in partner:
        pl.semaphore_signal(barrier, inc=1, device_id=p, device_id_type=MESH)

    @pl.loop(1, FSDP)
    def _(k):
        pl.semaphore_signal(barrier, inc=1, device_id=(c, lax.rem(f + k, FSDP)), device_id_type=MESH)

    small = [
        pltpu.make_async_copy(dexp_hbm.at[0, 0], dexp_v, in_sem.at[0]),
        pltpu.make_async_copy(signs_hbm, sv, in_sem.at[1]),
        pltpu.make_async_copy(signs_hbm.at[:, pl.ds(pl.multiple_of(f * OW, OW), OW)], so, in_sem.at[2]),
        pltpu.make_async_copy(master_hbm, master_v, in_sem.at[3]),
        pltpu.make_async_copy(mom_hbm, mom_v, in_sem.at[4]),
        pltpu.make_async_copy(mexp_hbm, mexp_v, in_sem.at[5]),
    ]
    loads = []
    for g, (start, n, _) in enumerate(GROUPS):
        cols = pl.ds(start * OW, n * OW)
        loads.append((
            pltpu.make_async_copy(local_hbm.at[0, 0, :, cols], lv.at[:, cols], ld_sem.at[g, 0]),
            pltpu.make_async_copy(outer_hbm.at[0, :, cols], ov.at[:, cols], ld_sem.at[g, 1]),
        ))
    small[0].start()
    small[1].start()
    for pair in loads:
        for cp in pair:
            cp.start()
    for cp in small[2:]:
        cp.start()

    table = sylvester(HB)
    table_b = table.astype(jnp.bfloat16)
    w1[0:HB, :] = table_b
    w1[HB:OW, :] = (-table).astype(jnp.bfloat16)
    zero = jnp.zeros((HB, HB), jnp.bfloat16)
    bd[0:HB, 0:HB] = table_b
    bd[HB:OW, HB:OW] = table_b
    bd[0:HB, HB:OW] = zero
    bd[HB:OW, 0:HB] = zero

    small[0].wait()
    thr[...] = power(dexp_v[...]).astype(jnp.float32) * LIMIT
    small[1].wait()

    def deltas(g, half):
        start, n, order = GROUPS[g]

        def block(j, carry):
            row = first_row(order, (half, lax.div(j, 2), lax.rem(j, 2)))
            tiles = []
            for k in range(2 * n):
                cols = pl.ds((2 * start + k) * HB, HB)
                flips = (1 - 2 * sv[:, cols]).astype(jnp.float32).astype(jnp.bfloat16)
                o = ov[pl.ds(row, RB), cols] * flips
                l = lv[pl.ds(row, RB), cols] * flips
                tiles.append(jnp.concatenate([o, l], axis=1))
            turned = jnp.dot(jnp.concatenate(tiles, axis=0), w1[...], preferred_element_type=jnp.float32)
            limits = thr[pl.ds(row, RB), :]
            for k in range(2 * n):
                cb = 2 * start + k
                top = jnp.broadcast_to(limits[:, cb:cb + 1], (RB, HB))
                value = turned[k * RB:(k + 1) * RB, :]
                value = jnp.minimum(jnp.maximum(value, -top), top)
                parts[g][half, j, :, pl.ds(k * HB, HB)] = value.astype(jnp.bfloat16)
            return carry

        lax.fori_loop(0, 4, block, 0)

    def remote(src, dst, send, recv, to):
        return pltpu.make_async_remote_copy(
            src_ref=src, dst_ref=dst, send_sem=send, recv_sem=recv, device_id=to, device_id_type=MESH
        )

    def rs_copy(g, step):
        to = partner[GROUPS[g][2][step]]
        src = (parts[g].at[1], parts[g].at[0, pl.ds(2, 2)], parts[g].at[0, 1])[step]
        dst = (r1[g], r2[g], r3[g])[step]
        return remote(src, dst, rs_send.at[g, step], rs_recv.at[g, step], to)

    def ag_copy(g, step):
        to = partner[GROUPS[g][2][2 - step]]
        src = (res[g].at[0, 0], res[g].at[0, pl.ds(0, 2)], res[g].at[0])[step]
        dst = (res[g].at[0, 1], res[g].at[0, pl.ds(2, 2)], res[g].at[1])[step]
        return remote(src, dst, ag_send.at[g, step], ag_recv.at[g, step], to)

    def add(mine, other):
        return mine.astype(jnp.float32) + other.astype(jnp.float32)

    for g in range(NG):
        for cp in loads[g]:
            cp.wait()
        deltas(g, 1)
        if g == 0:
            pl.semaphore_wait(barrier, 3 + FSDP - 1)
        rs_copy(g, 0).start()

    for cp in small[2:]:
        cp.wait()
    own = (1 - 2 * so[...]).astype(jnp.float32)

    def prepare(k, carry):
        s = pl.ds(k * 8, 8)
        a = (master_v[s] - KEEP_MOMENTUM * mom_v[s]).reshape(8 * RB, OW) * own
        hi = a.astype(jnp.bfloat16)
        lo = (a - hi.astype(jnp.float32)).astype(jnp.bfloat16)
        turned = jnp.dot(hi, bd[...], preferred_element_type=jnp.float32)
        turned += jnp.dot(lo, bd[...], preferred_element_type=jnp.float32)
        asrc[s, :, 0:OW] = turned.astype(jnp.bfloat16).reshape(8, RB, OW)
        e = mexp_v[s]
        first = lax.broadcasted_iota(jnp.int32, (8, RB, HB), 2) < HB // 2
        both = jnp.where(first, e[:, :, 0:1], e[:, :, 1:2])
        asrc[s, :, OW:OW + HB] = power(both)
        return carry

    lax.fori_loop(0, FSDP // 8, prepare, 0)

    @pl.loop(1, FSDP)
    def _(k):
        to = lax.rem(f + k, FSDP)
        remote(asrc.at[to], abuf.at[f], a1_sem.at[0], a1_sem.at[1], (c, to)).start()

    abuf[f] = asrc[f]

    for g in range(NG):
        deltas(g, 0)

    for g in range(NG):
        rs_copy(g, 0).wait_recv()

        def acc1(j, carry):
            parts[g][0, j] = add(parts[g][0, j], r1[g][j]).astype(jnp.bfloat16)
            return carry

        lax.fori_loop(2, 4, acc1, 0)
        rs_copy(g, 1).start()
        lax.fori_loop(0, 2, acc1, 0)
    for g in range(NG):
        rs_copy(g, 1).wait_recv()
        parts[g][0, 1] = add(parts[g][0, 1], r2[g][1]).astype(jnp.bfloat16)
        rs_copy(g, 2).start()
        parts[g][0, 0] = add(parts[g][0, 0], r2[g][0]).astype(jnp.bfloat16)

    whole = pl.ds(0, FSDP - 1)
    pltpu.make_async_copy(abuf.at[whole], abuf.at[whole], a1_sem.at[1]).wait()

    for g, (start, n, order) in enumerate(GROUPS):
        rs_copy(g, 2).wait_recv()
        codes = []
        for k in range(n):
            cols = pl.ds(k * OW, OW)
            total = add(parts[g][0, 0, :, cols], r3[g][:, cols])
            sbuf[start + k] = total.astype(jnp.bfloat16)
            code = abuf[start + k, :, 0:OW].astype(jnp.float32) - (GRAD_IN_MASTER / CUTS) * total
            scale = abuf[start + k, :, OW:OW + HB].astype(jnp.float32) * LIMIT
            top = jnp.concatenate(
                [jnp.broadcast_to(scale[:, 0:1], (RB, HB)), jnp.broadcast_to(scale[:, HB // 2:HB // 2 + 1], (RB, HB))],
                axis=1,
            )
            codes.append(jnp.minimum(jnp.maximum(code, -top), top).astype(jnp.bfloat16))
        turned = jnp.dot(jnp.concatenate(codes, axis=0), bd[...], preferred_element_type=jnp.float32)
        for k in range(n):
            flips = (1 - 2 * sv[:, pl.ds((start + k) * OW, OW)]).astype(jnp.float32) * (1.0 / HB)
            value = turned[k * RB:(k + 1) * RB, :] * flips
            res[g][0, 0, :, pl.ds(k * OW, OW)] = value.astype(jnp.bfloat16)
        ag_copy(g, 0).start()

        @pl.loop(start, start + n)
        def _(to):
            @pl.when(to != f)
            def _():
                remote(sbuf.at[to], srecv.at[f], a2_sem.at[0], a2_sem.at[1], (c, to)).start()

    srecv[f] = sbuf[f]

    def write(g, half, j):
        start, n, order = GROUPS[g]
        row = first_row(order, (half, j // 2, j % 2))
        return pltpu.make_async_copy(
            res[g].at[half, j],
            out_hbm.at[0, pl.ds(row, RB), pl.ds(start * OW, n * OW)],
            out_sem.at[g, half * 4 + j],
        )

    for g in range(NG):
        ag_copy(g, 0).wait_recv()
        ag_copy(g, 1).start()
        write(g, 0, 0).start()
        write(g, 0, 1).start()
    for g in range(NG):
        ag_copy(g, 1).wait_recv()
        ag_copy(g, 2).start()
        write(g, 0, 2).start()
        write(g, 0, 3).start()

    pltpu.make_async_copy(srecv.at[whole], srecv.at[whole], a2_sem.at[1]).wait()

    def finish(k, carry):
        s = pl.ds(k * 8, 8)
        turned = jnp.dot(srecv[s].reshape(8 * RB, OW), bd[...], preferred_element_type=jnp.float32)
        grad = (turned * (own * (1.0 / (HB * CUTS)))).reshape(8, RB, OW)
        mom = DECAY * mom_v[s] + grad
        mom_o[s] = mom
        master_o[s] = master_v[s] - OUTER_RATE * (grad + DECAY * mom)
        return carry

    lax.fori_loop(0, FSDP // 8, finish, 0)
    outs = [
        pltpu.make_async_copy(master_o, master_out, in_sem.at[0]),
        pltpu.make_async_copy(mom_o, mom_out, in_sem.at[1]),
    ]
    for cp in outs:
        cp.start()

    for g in range(NG):
        ag_copy(g, 2).wait_recv()
        for j in range(4):
            write(g, 1, j).start()
    for g in range(NG):
        for step in range(3):
            rs_copy(g, step).wait_send()
            ag_copy(g, step).wait_send()
        for half in range(2):
            for j in range(4):
                write(g, half, j).wait()
    pltpu.make_async_copy(asrc.at[whole], asrc.at[whole], a1_sem.at[0]).wait()
    pltpu.make_async_copy(sbuf.at[whole], sbuf.at[whole], a2_sem.at[0]).wait()
    for cp in outs:
        cp.wait()


def step(local_params, outer_params, column_signs, delta_exponents, outer_master, outer_momentum, master_exponents):
    bf16, f32, i32 = jnp.bfloat16, jnp.float32, jnp.int32
    widths = [n * OW for _, n, _ in GROUPS]
    anywhere = pl.BlockSpec(memory_space=pl.ANY)
    state = (FSDP, RB, OW)
    scratch = [
        pltpu.VMEM((ROWS, DIM), bf16),
        pltpu.VMEM((ROWS, DIM), bf16),
        pltpu.VMEM((1, DIM), i32),
        pltpu.VMEM((1, OW), i32),
        pltpu.VMEM((ROWS, DIM // HB), i32),
        pltpu.VMEM((ROWS, DIM // HB), f32),
        pltpu.VMEM(state, f32),
        pltpu.VMEM(state, f32),
        pltpu.VMEM((FSDP, RB, OW // HB), i32),
        pltpu.VMEM(state, f32),
        pltpu.VMEM(state, f32),
        pltpu.VMEM((OW, HB), bf16),
        pltpu.VMEM((OW, OW), bf16),
        pltpu.VMEM((FSDP, RB, OW + HB), bf16),
        pltpu.VMEM((FSDP, RB, OW + HB), bf16),
        pltpu.VMEM(state, bf16),
        pltpu.VMEM(state, bf16),
    ]
    scratch += [pltpu.VMEM((2, 4, RB, w), bf16) for w in widths]
    scratch += [pltpu.VMEM((4, RB, w), bf16) for w in widths]
    scratch += [pltpu.VMEM((2, RB, w), bf16) for w in widths]
    scratch += [pltpu.VMEM((RB, w), bf16) for w in widths]
    scratch += [pltpu.VMEM((2, 4, RB, w), bf16) for w in widths]
    dma = pltpu.SemaphoreType.DMA
    scratch += [
        dma((NG, 2)), dma((6,)), dma((NG, 3)), dma((NG, 3)), dma((NG, 3)), dma((NG, 3)),
        dma((2,)), dma((2,)), dma((NG, 8)),
    ]
    return pl.pallas_call(
        kernel,
        out_shape=(
            jax.ShapeDtypeStruct((1, ROWS, DIM), bf16),
            jax.ShapeDtypeStruct(state, f32),
            jax.ShapeDtypeStruct(state, f32),
        ),
        in_specs=[anywhere] * 7,
        out_specs=(anywhere,) * 3,
        scratch_shapes=scratch,
        compiler_params=pltpu.CompilerParams(
            collective_id=0, has_side_effects=True, vmem_limit_bytes=40 * 1024 * 1024
        ),
    )(
        local_params, outer_params, column_signs.reshape(1, DIM), delta_exponents,
        outer_master, outer_momentum, master_exponents,
    )


def solution(mesh):
    placed = (
        P("cuts", "fsdp", None, None),
        P("fsdp", None, None),
        P(),
        P("cuts", "fsdp", None, None),
        P(None, "cuts", "fsdp"),
        P(None, "cuts", "fsdp"),
        P(None, "cuts", "fsdp"),
    )
    return jax.shard_map(
        step,
        mesh=mesh,
        in_specs=placed,
        out_specs=(P("fsdp", None, None), P(None, "cuts", "fsdp"), P(None, "cuts", "fsdp")),
        check_vma=False,
    )
```

```python
import functools
import math

import jax
import jax.numpy as jnp
from jax import lax
from jax.experimental import pallas as pl
from jax.experimental.pallas import tpu as pltpu
from jax.sharding import PartitionSpec as P

HB = 128
RB = 16
OW = 256
CUTS = 8
FSDP = 32
DIM = FSDP * OW
ROWS = CUTS * RB
LIMIT = 448.0 * math.sqrt(HB)
OUTER_RATE = 0.7
DECAY = 0.9
KEEP_MOMENTUM = OUTER_RATE * DECAY * DECAY
GRAD_IN_MASTER = OUTER_RATE * (1.0 + DECAY)
MESH = pl.DeviceIdType.MESH

XA, XB, YH = 0, 1, 2
ORDERS = ((XA, XB, YH), (XB, YH, XA), (YH, XA, XB))
SIZES = (6, 5, 5, 6, 5, 5)


def column_groups():
    groups, start = [], 0
    for k, n in enumerate(SIZES):
        groups.append((start, n, ORDERS[k % 3]))
        start += n
    assert start == FSDP
    return groups


GROUPS = column_groups()
NG = len(GROUPS)


def sylvester(order):
    i = lax.broadcasted_iota(jnp.int32, (order, order), 0)
    j = lax.broadcasted_iota(jnp.int32, (order, order), 1)
    t = jnp.bitwise_and(i, j)
    for s in (4, 2, 1):
        t = jnp.bitwise_xor(t, jnp.right_shift(t, s))
    return (1 - 2 * jnp.bitwise_and(t, 1)).astype(jnp.float32)


def power(exponents):
    return jnp.exp2(exponents.astype(jnp.float32)).astype(jnp.bfloat16)


def kernel(
    local_hbm, outer_hbm, signs_hbm, dexp_hbm, master_hbm, mom_hbm, mexp_hbm,
    out_v, master_o, mom_o,
    lv, ov, sv, so, flips16, dexp_v, thr, master_v, mom_v, mexp_v,
    w1, bd, asrc, abuf, sbuf, srecv,
    *rest,
):
    parts, r1, r2, r3 = (rest[k * NG:(k + 1) * NG] for k in range(4))
    ld_sem, in_sem, rs_send, rs_recv, ag_send, ag_recv, a1_send, a1_recv, a2_sem, reply = rest[4 * NG:]
    c, f = lax.axis_index("cuts"), lax.axis_index("fsdp")
    x, yh = lax.div(c, 2), lax.rem(c, 2)
    v = lax.div(x, 2)
    u = lax.rem(lax.rem(x, 2) + v, 2)
    flip_x = x + 1 - 2 * lax.rem(x, 2)
    partner = (
        (flip_x * 2 + yh, f),
        ((3 - x) * 2 + yh, f),
        (x * 2 + 1 - yh, f),
    )

    def first_row(order, bits):
        mine = [u, v, yh]
        for d, b in zip(order, bits):
            mine[d] = lax.rem(mine[d] + b, 2)
        au, av, ay = mine
        ax = av * 2 + lax.rem(au + av, 2)
        return pl.multiple_of((ax * 2 + ay) * RB, RB)

    half = lax.div(f, FSDP // 2)

    def owner(q):
        return lax.rem(q + half * (FSDP // 2), FSDP)

    def at(q, n):
        return pl.ds(pl.multiple_of(owner(q) * OW, OW), n * OW)

    barrier = pltpu.get_barrier_semaphore()
    for p in partner:
        pl.semaphore_signal(barrier, inc=1, device_id=p, device_id_type=MESH)

    small = [
        pltpu.make_async_copy(signs_hbm.at[:, at(0, FSDP // 2)], sv.at[:, pl.ds(0, DIM // 2)], in_sem.at[0]),
        pltpu.make_async_copy(dexp_hbm.at[0, 0], dexp_v, in_sem.at[1]),
        pltpu.make_async_copy(master_hbm, master_v, in_sem.at[2]),
        pltpu.make_async_copy(mom_hbm, mom_v, in_sem.at[3]),
        pltpu.make_async_copy(mexp_hbm, mexp_v, in_sem.at[4]),
        pltpu.make_async_copy(signs_hbm.at[:, pl.ds(pl.multiple_of(f * OW, OW), OW)], so, in_sem.at[5]),
        pltpu.make_async_copy(signs_hbm.at[:, at(FSDP // 2, FSDP // 2)], sv.at[:, pl.ds(DIM // 2, DIM // 2)], in_sem.at[6]),
    ]
    loads = []
    for g, (start, n, _) in enumerate(GROUPS):
        cols = pl.ds(start * OW, n * OW)
        loads.append((
            pltpu.make_async_copy(local_hbm.at[0, 0, :, at(start, n)], lv.at[:, cols], ld_sem.at[g, 0]),
            pltpu.make_async_copy(outer_hbm.at[0, :, at(start, n)], ov.at[:, cols], ld_sem.at[g, 1]),
        ))
    small[0].start()
    small[1].start()
    small[6].start()
    for pair in loads:
        for cp in pair:
            cp.start()
    for cp in small[2:6]:
        cp.start()

    @pl.loop(f + 1, FSDP)
    def _(to):
        pl.semaphore_signal(barrier, inc=1, device_id=(c, to), device_id_type=MESH)

    table = sylvester(HB)
    table_b = table.astype(jnp.bfloat16)
    w1[0:HB, :] = table_b
    w1[HB:OW, :] = (-table).astype(jnp.bfloat16)
    zero = jnp.zeros((HB, HB), jnp.bfloat16)
    bd[0:HB, 0:HB] = table_b
    bd[HB:OW, HB:OW] = table_b
    bd[0:HB, HB:OW] = zero
    bd[HB:OW, 0:HB] = zero

    small[0].wait()
    small[6].wait()
    for k in range(DIM // OW):
        cols = pl.ds(k * OW, OW)
        row = (1 - 2 * sv[:, cols]).astype(jnp.float32)
        flips16[:, cols] = jnp.broadcast_to(row, (RB, OW)).astype(jnp.bfloat16)
    small[1].wait()
    limits = (power(dexp_v[...]).astype(jnp.float32) * LIMIT).T
    swapped = jnp.concatenate([limits[:, DIM // HB // 2:], limits[:, :DIM // HB // 2]], axis=1)
    thr[...] = jnp.where(half == 0, limits, swapped)

    def deltas(g, part):
        start, n, order = GROUPS[g]
        rows = [first_row(order, (part, j // 2, j % 2)) for j in range(4)]
        tiles = []
        for row in rows:
            for k in range(2 * n):
                cols = pl.ds((2 * start + k) * HB, HB)
                flips = flips16[:, cols]
                o = ov[pl.ds(row, RB), cols] * flips
                l = lv[pl.ds(row, RB), cols] * flips
                tiles.append(jnp.concatenate([o, l], axis=1))
        turned = jnp.dot(jnp.concatenate(tiles, axis=0), w1[...], preferred_element_type=jnp.float32)
        for j, row in enumerate(rows):
            limits = thr[pl.ds(row, RB), :]
            for k in range(2 * n):
                cb = 2 * start + k
                top = jnp.broadcast_to(limits[:, cb:cb + 1], (RB, HB))
                at_row = (j * 2 * n + k) * RB
                value = turned[at_row:at_row + RB, :]
                value = jnp.minimum(jnp.maximum(value, -top), top)
                parts[g][part, j, :, pl.ds(k * HB, HB)] = value.astype(jnp.bfloat16)

    def remote(src, dst, send, recv, to):
        return pltpu.make_async_remote_copy(
            src_ref=src, dst_ref=dst, send_sem=send, recv_sem=recv, device_id=to, device_id_type=MESH
        )

    def rs_copy(g, i):
        to = partner[GROUPS[g][2][(0, 0, 1, 1, 2)[i]]]
        two = (pl.ds(2, 2), pl.ds(0, 2))
        src = (
            lambda: parts[g].at[1, two[0]], lambda: parts[g].at[1, two[1]],
            lambda: parts[g].at[0, 3], lambda: parts[g].at[0, 2], lambda: parts[g].at[0, 1],
        )[i]()
        dst = (
            lambda: r1[g].at[two[0]], lambda: r1[g].at[two[1]],
            lambda: r2[g].at[1], lambda: r2[g].at[0], lambda: r3[g],
        )[i]()
        return remote(src, dst, rs_send.at[g, i], rs_recv.at[g, i], to)

    def ag_copy(g, d, i):
        start, n, order = GROUPS[g]
        row = first_row(order, (0, i // 2, i % 2))
        block = out_v.at[pl.ds(row, RB), at(start, n)]
        slot = (0, 4, 6)[d] + i
        return remote(block, block, ag_send.at[g, slot], ag_recv.at[g, slot], partner[order[d]])

    def add(mine, other):
        return mine.astype(jnp.float32) + other.astype(jnp.float32)

    early, late = range(0, NG // 2), range(NG // 2, NG)
    for g in early:
        for cp in loads[g]:
            cp.wait()
        deltas(g, 1)
        if g == 0:
            pl.semaphore_wait(barrier, 3 + f)
        rs_copy(g, 0).start()
        rs_copy(g, 1).start()
        if g == 0:
            @pl.loop(0, f)
            def _(to):
                other = half - lax.div(to, FSDP // 2)
                pl.semaphore_signal(reply.at[other], inc=1, device_id=(c, to), device_id_type=MESH)

    for cp in small[2:6]:
        cp.wait()
    own = (1 - 2 * so[...]).astype(jnp.float32)

    def prepare(k, carry):
        s = pl.ds(k * 8, 8)
        a = (master_v[s] - KEEP_MOMENTUM * mom_v[s]).reshape(8 * RB, OW) * own
        hi = a.astype(jnp.bfloat16)
        lo = (a - hi.astype(jnp.float32)).astype(jnp.bfloat16)
        turned = jnp.dot(hi, bd[...], preferred_element_type=jnp.float32)
        turned += jnp.dot(lo, bd[...], preferred_element_type=jnp.float32)
        asrc[s, :, 0:OW] = turned.astype(jnp.bfloat16).reshape(8, RB, OW)
        return carry

    lax.fori_loop(0, FSDP // 8, prepare, 0)
    scales = [power(mexp_v[:, b, :]).astype(jnp.float32) for b in range(2)]
    first = lax.broadcasted_iota(jnp.int32, (RB, HB), 1) < HB // 2
    for s in range(FSDP):
        both = jnp.where(
            first,
            jnp.broadcast_to(scales[0][:, s:s + 1], (RB, HB)),
            jnp.broadcast_to(scales[1][:, s:s + 1], (RB, HB)),
        )
        asrc[s, :, OW:OW + HB] = both.astype(jnp.bfloat16)

    def owner_copy(to):
        return remote(asrc.at[to], abuf.at[f], a1_send, a1_recv.at[f], (c, to))

    def owner_send(low, high):
        @pl.loop(low, high)
        def _(to):
            owner_copy(to).start()

    owner_send(0, f)
    abuf[f] = asrc[f]

    for g in early:
        deltas(g, 0)
    for g in late:
        for cp in loads[g]:
            cp.wait()
        deltas(g, 1)

    def acc1(g, low):
        def one(j, carry):
            parts[g][0, j] = add(parts[g][0, j], r1[g][j]).astype(jnp.bfloat16)
            return carry

        lax.fori_loop(low, low + 2, one, 0)

    def stage_a(groups):
        for g in groups:
            rs_copy(g, 0).wait_recv()
            acc1(g, 2)
            rs_copy(g, 2).start()
            rs_copy(g, 3).start()

    def stage_b(groups):
        for g in groups:
            rs_copy(g, 1).wait_recv()
            acc1(g, 0)

    def stage_c(groups):
        for g in groups:
            rs_copy(g, 2).wait_recv()
            parts[g][0, 1] = add(parts[g][0, 1], r2[g][1]).astype(jnp.bfloat16)
            rs_copy(g, 4).start()

    def stage_d(groups):
        for g in groups:
            rs_copy(g, 3).wait_recv()
            parts[g][0, 0] = add(parts[g][0, 0], r2[g][0]).astype(jnp.bfloat16)

    def stage_e(groups):
        for g in groups:
            start, n, order = GROUPS[g]
            rs_copy(g, 4).wait_recv()

            @pl.loop(start, start + n)
            def _(q):
                s = owner(q)

                @pl.when(s != f)
                def _():
                    remote(asrc.at[s], abuf.at[s], a1_send, a1_recv.at[s], (c, s)).wait_recv()

            codes = []
            for k in range(n):
                cols = pl.ds(k * OW, OW)
                s = owner(start + k)
                total = add(parts[g][0, 0, :, cols], r3[g][:, cols])
                sbuf[s] = total.astype(jnp.bfloat16)
                code = abuf[s, :, 0:OW].astype(jnp.float32) - (GRAD_IN_MASTER / CUTS) * total
                scale = abuf[s, :, OW:OW + HB].astype(jnp.float32) * LIMIT
                top = jnp.concatenate(
                    [jnp.broadcast_to(scale[:, b:b + 1], (RB, HB)) for b in (0, HB // 2)], axis=1
                )
                codes.append(jnp.minimum(jnp.maximum(code, -top), top).astype(jnp.bfloat16))
            turned = jnp.dot(jnp.concatenate(codes, axis=0), bd[...], preferred_element_type=jnp.float32)
            row = first_row(order, (0, 0, 0))
            for k in range(n):
                flips = flips16[:, pl.ds((start + k) * OW, OW)].astype(jnp.float32) * (1.0 / HB)
                out_v[pl.ds(row, RB), at(start + k, 1)] = (turned[k * RB:(k + 1) * RB, :] * flips).astype(jnp.bfloat16)
            for d in (2, 1, 0):
                ag_copy(g, d, 0).start()

            @pl.loop(start, start + n)
            def _(q):
                to = owner(q)

                @pl.when(to != f)
                def _():
                    remote(sbuf.at[to], srecv.at[f], a2_sem.at[0], a2_sem.at[1], (c, to)).start()

    def forward1(groups):
        for g in groups:
            ag_copy(g, 2, 0).wait_recv()
            ag_copy(g, 1, 1).start()
            ag_copy(g, 0, 1).start()

    def forward2(groups):
        for g in groups:
            for i in range(2):
                ag_copy(g, 1, i).wait_recv()
                ag_copy(g, 0, 2 + i).start()

    stage_a(early)
    for g in late:
        rs_copy(g, 0).start()
    split = (half + 1) * (FSDP // 2)

    @pl.when(f + 1 < split)
    def _():
        pl.semaphore_wait(reply.at[0], split - 1 - f)
        owner_send(f + 1, split)

    stage_b(early)
    stage_c(early)
    for g in late:
        rs_copy(g, 1).start()
    for g in late:
        deltas(g, 0)
    stage_d(early)
    stage_a(late)
    stage_e(early)

    @pl.when(split < FSDP)
    def _():
        pl.semaphore_wait(reply.at[1], FSDP - split)
        owner_send(split, FSDP)

    stage_b(late)
    stage_c(late)
    stage_d(late)
    forward1(early)
    stage_e(late)
    forward2(early)
    srecv[f] = sbuf[f]
    forward1(late)
    forward2(late)

    others = pl.ds(0, FSDP - 1)
    pltpu.make_async_copy(srecv.at[others], srecv.at[others], a2_sem.at[1]).wait()

    def finish(k, carry):
        s = pl.ds(k * 8, 8)
        turned = jnp.dot(srecv[s].reshape(8 * RB, OW), bd[...], preferred_element_type=jnp.float32)
        grad = (turned * (own * (1.0 / (HB * CUTS)))).reshape(8, RB, OW)
        mom = DECAY * mom_v[s] + grad
        mom_o[s] = mom
        master_o[s] = master_v[s] - OUTER_RATE * (grad + DECAY * mom)
        return carry

    lax.fori_loop(0, FSDP // 8, finish, 0)

    for g in range(NG):
        for i in range(4):
            ag_copy(g, 0, i).wait_recv()
    for g in range(NG):
        for i in range(5):
            rs_copy(g, i).wait_send()
        for d in range(3):
            for i in range((4, 2, 1)[d]):
                ag_copy(g, d, i).wait_send()
    pltpu.make_async_copy(asrc.at[others], asrc.at[others], a1_send).wait()
    pltpu.make_async_copy(sbuf.at[others], sbuf.at[others], a2_sem.at[0]).wait()


def write_out(out_v, master_v, mom_v, out_hbm, master_hbm, mom_hbm, sem):
    copies = [
        pltpu.make_async_copy(out_v.at[pl.ds(k * 32, 32)], out_hbm.at[0, pl.ds(k * 32, 32)], sem.at[k]) for k in range(4)
    ]
    copies += [
        pltpu.make_async_copy(master_v, master_hbm, sem.at[4]),
        pltpu.make_async_copy(mom_v, mom_hbm, sem.at[5]),
    ]
    for cp in copies:
        cp.start()
    for cp in copies:
        cp.wait()


def step(local_params, outer_params, column_signs, delta_exponents, outer_master, outer_momentum, master_exponents):
    bf16, f32, i32 = jnp.bfloat16, jnp.float32, jnp.int32
    widths = [n * OW for _, n, _ in GROUPS]
    anywhere = pl.BlockSpec(memory_space=pl.ANY)
    vmem = pl.BlockSpec(memory_space=pltpu.VMEM)
    state = (FSDP, RB, OW)
    scratch = [
        pltpu.VMEM((ROWS, DIM), bf16),
        pltpu.VMEM((ROWS, DIM), bf16),
        pltpu.VMEM((1, DIM), i32),
        pltpu.VMEM((1, OW), i32),
        pltpu.VMEM((RB, DIM), bf16),
        pltpu.VMEM((DIM // HB, ROWS), i32),
        pltpu.VMEM((ROWS, DIM // HB), f32),
        pltpu.VMEM(state, f32),
        pltpu.VMEM(state, f32),
        pltpu.VMEM((RB, OW // HB, FSDP), i32),
        pltpu.VMEM((OW, HB), bf16),
        pltpu.VMEM((OW, OW), bf16),
        pltpu.VMEM((FSDP, RB, OW + HB), bf16),
        pltpu.VMEM((FSDP, RB, OW + HB), bf16),
        pltpu.VMEM(state, bf16),
        pltpu.VMEM(state, bf16),
    ]
    scratch += [pltpu.VMEM((2, 4, RB, w), bf16) for w in widths]
    scratch += [pltpu.VMEM((4, RB, w), bf16) for w in widths]
    scratch += [pltpu.VMEM((2, RB, w), bf16) for w in widths]
    scratch += [pltpu.VMEM((RB, w), bf16) for w in widths]
    dma = pltpu.SemaphoreType.DMA
    scratch += [
        dma((NG, 2)), dma((7,)), dma((NG, 5)), dma((NG, 5)), dma((NG, 7)), dma((NG, 7)),
        dma, dma((FSDP,)), dma((2,)), pltpu.SemaphoreType.REGULAR((2,)),
    ]
    hbm = functools.partial(pltpu.with_memory_space_constraint, memory_space=pltpu.HBM)
    held = pl.pallas_call(
        kernel,
        out_shape=(pltpu.VMEM((ROWS, DIM), bf16), pltpu.VMEM(state, f32), pltpu.VMEM(state, f32)),
        in_specs=[anywhere] * 7,
        out_specs=(vmem,) * 3,
        scratch_shapes=scratch,
        compiler_params=pltpu.CompilerParams(
            collective_id=0, has_side_effects=True, vmem_limit_bytes=40 * 1024 * 1024
        ),
    )(
        hbm(local_params), hbm(outer_params), hbm(column_signs.reshape(1, DIM)),
        hbm(jnp.swapaxes(delta_exponents, 2, 3)), hbm(outer_master), hbm(outer_momentum),
        hbm(jnp.transpose(master_exponents, (1, 2, 0))),
    )
    return pl.pallas_call(
        write_out,
        out_shape=(
            pltpu.HBM((1, ROWS, DIM), bf16),
            pltpu.HBM(state, f32),
            pltpu.HBM(state, f32),
        ),
        in_specs=[vmem] * 3,
        out_specs=(anywhere,) * 3,
        scratch_shapes=[dma((6,))],
    )(*[pltpu.with_memory_space_constraint(h, pltpu.VMEM) for h in held])


def solution(mesh):
    placed = (
        P("cuts", "fsdp", None, None),
        P("fsdp", None, None),
        P(),
        P("cuts", "fsdp", None, None),
        P(None, "cuts", "fsdp"),
        P(None, "cuts", "fsdp"),
        P(None, "cuts", "fsdp"),
    )
    return jax.shard_map(
        step,
        mesh=mesh,
        in_specs=placed,
        out_specs=(P("fsdp", None, None), P(None, "cuts", "fsdp"), P(None, "cuts", "fsdp")),
        check_vma=False,
    )
```

```python
import functools
import math

import jax
import jax.numpy as jnp
from jax import lax
from jax.experimental import pallas as pl
from jax.experimental.pallas import tpu as pltpu
from jax.sharding import PartitionSpec as P

HB = 128
RB = 16
OW = 256
CUTS = 8
FSDP = 32
DIM = FSDP * OW
ROWS = CUTS * RB
LIMIT = 448.0 * math.sqrt(HB)
OUTER_RATE = 0.7
DECAY = 0.9
KEEP_MOMENTUM = OUTER_RATE * DECAY * DECAY
GRAD_IN_MASTER = OUTER_RATE * (1.0 + DECAY)
MESH = pl.DeviceIdType.MESH

XA, XB, YH = 0, 1, 2
ORDERS = ((XA, XB, YH), (XB, YH, XA), (YH, XA, XB))
SIZES = (6, 6, 4, 6, 4, 6)
PEERS = FSDP // 2


def column_groups():
    groups, start = [], 0
    for k, n in enumerate(SIZES):
        groups.append((start, n, k // 3, ORDERS[k % 3]))
        start += n
    assert start == FSDP
    return groups


GROUPS = column_groups()
NG = len(GROUPS)
EARLY, LATE = range(0, NG // 2), range(NG // 2, NG)


def y_weight(g):
    _, _, cross, order = GROUPS[g]
    return (4, 2, 1)[order.index(YH)] if cross else 0


def bits(i):
    return (i // 4, i // 2 % 2, i % 2)


def sylvester(order):
    i = lax.broadcasted_iota(jnp.int32, (order, order), 0)
    j = lax.broadcasted_iota(jnp.int32, (order, order), 1)
    t = jnp.bitwise_and(i, j)
    for s in (4, 2, 1):
        t = jnp.bitwise_xor(t, jnp.right_shift(t, s))
    return (1 - 2 * jnp.bitwise_and(t, 1)).astype(jnp.float32)


def power(exponents):
    return jnp.exp2(exponents.astype(jnp.float32)).astype(jnp.bfloat16)


def kernel(
    local_hbm, outer_hbm, signs_hbm, dexp_hbm, master_hbm, mom_hbm, mexp_hbm,
    out_v, master_o, mom_o,
    lv, ov, sv, so, flips16, dexp_v, thr, master_v, mom_v, mexp_v,
    w1, bd, asrc, abuf, sbuf, srecv,
    *rest,
):
    parts, r1, r2, r3 = (rest[k * NG:(k + 1) * NG] for k in range(4))
    rest = rest[4 * NG:]
    rx = dict(zip(LATE, rest[:len(LATE)]))
    side = dict(zip(LATE, rest[len(LATE):2 * len(LATE)]))
    ld_sem, in_sem, rs_send, rs_recv, ag_send, ag_recv, a1_send, a1_recv, a2_sem, reply = rest[2 * len(LATE):]
    c, f = lax.axis_index("cuts"), lax.axis_index("fsdp")
    x, yh = lax.div(c, 2), lax.rem(c, 2)
    z, yl, core = lax.div(f, 4), lax.rem(lax.div(f, 2), 2), lax.rem(f, 2)
    v = lax.div(x, 2)
    u = lax.rem(lax.rem(x, 2) + v, 2)
    flip_x = x + 1 - 2 * lax.rem(x, 2)
    sister = z * 4 + (1 - yl) * 2 + core
    partner = (
        (flip_x * 2 + yh, f),
        ((3 - x) * 2 + yh, f),
        (x * 2 + 1 - yh, f),
    )
    near, far = (c, sister), (x * 2 + 1 - yh, sister)
    place = z * 2 + core
    half = lax.div(place, PEERS // 2)

    def peer(m):
        return (c, lax.div(m, 2) * 4 + yl * 2 + lax.rem(m, 2))

    def member(q):
        return lax.rem(q % PEERS // 2 + half * 4, 8) * 2 + q % 2

    def line(q):
        return pl.ds(pl.multiple_of(member(q) * 2 * OW + lax.rem(yl + q // PEERS, 2) * 2 * OW, 2 * OW), 2 * OW)

    def first_row(order, flips):
        mine = [u, v, yh]
        for d, b in zip(order, flips):
            mine[d] = lax.rem(mine[d] + b, 2)
        au, av, ay = mine
        ax = av * 2 + lax.rem(au + av, 2)
        return pl.multiple_of((ax * 2 + ay) * RB, RB)

    barrier = pltpu.get_barrier_semaphore()
    for p in (*partner, near, far):
        pl.semaphore_signal(barrier, inc=1, device_id=p, device_id_type=MESH)

    small = [
        pltpu.make_async_copy(signs_hbm, sv, in_sem.at[0]),
        pltpu.make_async_copy(dexp_hbm.at[0, 0], dexp_v, in_sem.at[1]),
        pltpu.make_async_copy(master_hbm, master_v, in_sem.at[2]),
        pltpu.make_async_copy(mom_hbm, mom_v, in_sem.at[3]),
        pltpu.make_async_copy(mexp_hbm, mexp_v, in_sem.at[4]),
        pltpu.make_async_copy(signs_hbm.at[:, pl.ds(pl.multiple_of(f * OW, OW), OW)], so, in_sem.at[5]),
    ]
    loads = []
    for q in range(0, FSDP, 2):
        cols, source = pl.ds(q * OW, 2 * OW), line(q)
        loads.append((
            pltpu.make_async_copy(local_hbm.at[0, 0, :, source], lv.at[:, cols], ld_sem.at[q // 2, 0]),
            pltpu.make_async_copy(outer_hbm.at[0, :, source], ov.at[:, cols], ld_sem.at[q // 2, 1]),
        ))
    small[0].start()
    small[1].start()
    for pair in loads[:PEERS // 2]:
        for cp in pair:
            cp.start()
    for cp in small[2:]:
        cp.start()
    for pair in loads[PEERS // 2:]:
        for cp in pair:
            cp.start()

    @pl.loop(place + 1, PEERS)
    def _(m):
        pl.semaphore_signal(barrier, inc=1, device_id=peer(m), device_id_type=MESH)

    table = sylvester(HB)
    table_b = table.astype(jnp.bfloat16)
    w1[0:HB, :] = table_b
    w1[HB:OW, :] = (-table).astype(jnp.bfloat16)
    zero = jnp.zeros((HB, HB), jnp.bfloat16)
    bd[0:HB, 0:HB] = table_b
    bd[HB:OW, HB:OW] = table_b
    bd[0:HB, HB:OW] = zero
    bd[HB:OW, 0:HB] = zero

    small[0].wait()
    for q in range(0, FSDP, 2):
        row = (1 - 2 * sv[:, line(q)]).astype(jnp.float32)
        flips16[:, pl.ds(q * OW, 2 * OW)] = jnp.broadcast_to(row, (RB, 2 * OW)).astype(jnp.bfloat16)
    blocks = DIM // HB
    block = lax.broadcasted_iota(jnp.int32, (blocks, blocks), 0)
    spot = lax.broadcasted_iota(jnp.int32, (blocks, blocks), 1)
    cross = jnp.bitwise_and(jnp.right_shift(spot, 5) + yl, 1)
    wanted = jnp.bitwise_and(jnp.right_shift(spot, 2) + half * 4, 7) * 8 + cross * 4 + jnp.bitwise_and(spot, 3)
    move = jnp.where(block == wanted, 1.0, 0.0).astype(jnp.bfloat16)
    small[1].wait()
    powers = power(dexp_v[...]).astype(jnp.float32).T.astype(jnp.bfloat16)
    thr[...] = jnp.dot(powers, move, preferred_element_type=jnp.float32) * LIMIT

    def deltas(g, part):
        start, n, _, order = GROUPS[g]
        rows = [first_row(order, (part, j // 2, j % 2)) for j in range(4)]
        tiles = []
        for row in rows:
            for k in range(2 * n):
                cols = pl.ds((2 * start + k) * HB, HB)
                flips = flips16[:, cols]
                o = ov[pl.ds(row, RB), cols] * flips
                l = lv[pl.ds(row, RB), cols] * flips
                tiles.append(jnp.concatenate([o, l], axis=1))
        turned = jnp.dot(jnp.concatenate(tiles, axis=0), w1[...], preferred_element_type=jnp.float32)
        for j, row in enumerate(rows):
            limits = thr[pl.ds(row, RB), :]
            for k in range(2 * n):
                cb = 2 * start + k
                top = jnp.broadcast_to(limits[:, cb:cb + 1], (RB, HB))
                at_row = (j * 2 * n + k) * RB
                value = turned[at_row:at_row + RB, :]
                value = jnp.minimum(jnp.maximum(value, -top), top)
                parts[g][part, j, :, pl.ds(k * HB, HB)] = value.astype(jnp.bfloat16)

    def load(g):
        start, n, _, _ = GROUPS[g]
        for pair in loads[start // 2:(start + n) // 2]:
            for cp in pair:
                cp.wait()

    def remote(src, dst, send, recv, to):
        return pltpu.make_async_remote_copy(
            src_ref=src, dst_ref=dst, send_sem=send, recv_sem=recv, device_id=to, device_id_type=MESH
        )

    def kept1(g, j):
        return rx[g].at[j] if y_weight(g) == 4 else parts[g].at[0, j]

    def kept2(g, j):
        return rx[g].at[j] if y_weight(g) == 2 else kept1(g, j)

    def kept3(g):
        return rx[g].at[0] if y_weight(g) == 1 else kept2(g, 0)

    def rs_copies(g, i):
        level = (0, 0, 1, 1, 2)[i]
        order = GROUPS[g][3]
        two = pl.ds((2, 0)[i], 2) if i < 2 else None
        one = (None, None, 1, 0, None)[i]
        dst = (lambda: r1[g].at[two], lambda: r2[g].at[one], lambda: r3[g])[level]()
        sources = [
            (lambda: parts[g].at[b, two], lambda: kept1(g, 2 * b + one), lambda: kept2(g, b))[level]() for b in range(2)
        ]
        if y_weight(g) != (4, 2, 1)[level]:
            return [remote(sources[1], dst, rs_send.at[g, i], rs_recv.at[g, i], partner[order[level]])]
        other = (lambda: rx[g].at[two], lambda: rx[g].at[one], lambda: rx[g].at[0])[level]()
        return [
            remote(sources[1], dst, rs_send.at[g, i], rs_recv.at[g, i], far),
            remote(sources[0], other, rs_send.at[g, 5 + i], rs_recv.at[g, 5 + i], near),
        ]

    def rs_start(g, i):
        for cp in rs_copies(g, i):
            cp.start()

    def rs_wait(g, i):
        for cp in rs_copies(g, i):
            cp.wait_recv()

    def block_of(g, i):
        start, n, _, order = GROUPS[g]
        return out_v.at[pl.ds(first_row(order, bits(i)), RB), pl.ds(start * OW, n * OW)]

    def ag_slots(g, slot):
        return ag_send.at[g, slot], ag_recv.at[g, slot]

    def ag_from_side(g, i):
        yb, order = y_weight(g), GROUPS[g][3]
        found = []
        for w in (1, 2, 4):
            if i < w < yb:
                to = partner[order[{4: 0, 2: 1, 1: 2}[w]]]
                found.append(remote(side[g].at[i], side[g].at[i + w], *ag_slots(g, 8 + i + w), to))
        found.append(remote(side[g].at[i], block_of(g, i), *ag_slots(g, i), near))
        found.append(remote(side[g].at[i], block_of(g, i), *ag_slots(g, i + yb), far))
        return found

    def ag_from_block(g, i):
        yb, order = y_weight(g), GROUPS[g][3]
        found = []
        for w in (1, 2, 4):
            if w > i and w >= 2 * yb:
                to = partner[order[{4: 0, 2: 1, 1: 2}[w]]]
                found.append(remote(block_of(g, i), block_of(g, i), *ag_slots(g, i + w), to))
        return found

    def ag_arrive(g, slot):
        ref = side[g].at[slot - 8] if slot >= 8 else block_of(g, slot)
        remote(ref, ref, *ag_slots(g, slot), near).wait_recv()

    def ag_pass_on(g, slot):
        ag_arrive(g, slot)
        for cp in ag_from_side(g, slot - 8) if slot >= 8 else ag_from_block(g, slot):
            cp.start()

    def add(mine, other):
        return mine.astype(jnp.float32) + other.astype(jnp.float32)

    pl.semaphore_wait(barrier, 5 + place)

    @pl.loop(0, place)
    def _(m):
        other = half - lax.div(m, PEERS // 2)
        pl.semaphore_signal(reply.at[other], inc=1, device_id=peer(m), device_id_type=MESH)

    for g in EARLY:
        load(g)
        deltas(g, 1)
        rs_start(g, 0)
        rs_start(g, 1)

    for cp in small[2:]:
        cp.wait()
    own = (1 - 2 * so[...]).astype(jnp.float32)

    def prepare(k, carry):
        s = pl.ds(k * 8, 8)
        a = (master_v[s] - KEEP_MOMENTUM * mom_v[s]).reshape(8 * RB, OW) * own
        hi = a.astype(jnp.bfloat16)
        lo = (a - hi.astype(jnp.float32)).astype(jnp.bfloat16)
        turned = jnp.dot(hi, bd[...], preferred_element_type=jnp.float32)
        turned += jnp.dot(lo, bd[...], preferred_element_type=jnp.float32)
        turned = turned.astype(jnp.bfloat16)
        for t in range(8):
            to, which = k * 4 + t // 4 * 2 + t % 2, lax.rem(t // 2 % 2 + yl, 2)
            asrc[to, which, :, 0:OW] = turned[t * RB:(t + 1) * RB, :]
        return carry

    lax.fori_loop(0, FSDP // 8, prepare, 0)
    scales = [power(mexp_v[:, b, :]).astype(jnp.float32) for b in range(2)]
    first = lax.broadcasted_iota(jnp.int32, (RB, HB), 1) < HB // 2
    for s in range(FSDP):
        both = jnp.where(
            first,
            jnp.broadcast_to(scales[0][:, s:s + 1], (RB, HB)),
            jnp.broadcast_to(scales[1][:, s:s + 1], (RB, HB)),
        )
        to, which = s // 4 * 2 + s % 2, lax.rem(s // 2 % 2 + yl, 2)
        asrc[to, which, :, OW:OW + HB] = both.astype(jnp.bfloat16)

    def owner_send(low, high):
        @pl.loop(low, high)
        def _(m):
            remote(asrc.at[m], abuf.at[place], a1_send, a1_recv.at[place], peer(m)).start()

    owner_send(0, place)
    abuf[place] = asrc[place]

    for g in EARLY:
        deltas(g, 0)

    def stage_a(groups):
        for g in groups:
            rs_wait(g, 0)
            for j in (3, 2):
                kept1(g, j)[...] = add(kept1(g, j)[...], r1[g][j]).astype(jnp.bfloat16)
            if y_weight(g) != 2:
                rs_start(g, 2)
                rs_start(g, 3)

    def stage_b(groups):
        for g in groups:
            rs_wait(g, 1)
            for j in (1, 0):
                kept1(g, j)[...] = add(kept1(g, j)[...], r1[g][j]).astype(jnp.bfloat16)
            if y_weight(g) == 2:
                rs_start(g, 2)
                rs_start(g, 3)

    def stage_c(groups):
        for g in groups:
            rs_wait(g, 2)
            kept2(g, 1)[...] = add(kept2(g, 1)[...], r2[g][1]).astype(jnp.bfloat16)
            if y_weight(g) != 1:
                rs_start(g, 4)

    def stage_d(groups):
        for g in groups:
            rs_wait(g, 3)
            kept2(g, 0)[...] = add(kept2(g, 0)[...], r2[g][0]).astype(jnp.bfloat16)
            if y_weight(g) == 1:
                rs_start(g, 4)

    def stage_e(groups):
        for g in groups:
            start, n, cross, order = GROUPS[g]
            low = start % PEERS
            rs_wait(g, 4)
            if not cross:
                for k in range(n):
                    m = member(low + k)

                    @pl.when(m != place)
                    def _():
                        remote(asrc.at[m], abuf.at[m], a1_send, a1_recv.at[m], peer(m)).wait_recv()

            codes = []
            for k in range(n):
                cols = pl.ds(k * OW, OW)
                total = add(kept3(g)[:, cols], r3[g][:, cols])
                m = member(low + k)
                sbuf[m, cross] = total.astype(jnp.bfloat16)
                code = abuf[m, cross, :, 0:OW].astype(jnp.float32) - (GRAD_IN_MASTER / CUTS) * total
                scale = abuf[m, cross, :, OW:OW + HB].astype(jnp.float32) * LIMIT
                top = jnp.concatenate(
                    [jnp.broadcast_to(scale[:, b:b + 1], (RB, HB)) for b in (0, HB // 2)], axis=1
                )
                codes.append(jnp.minimum(jnp.maximum(code, -top), top).astype(jnp.bfloat16))
            turned = jnp.dot(jnp.concatenate(codes, axis=0), bd[...], preferred_element_type=jnp.float32)
            row = first_row(order, (0, 0, 0))
            for k in range(n):
                flips = flips16[:, pl.ds((low + k) * OW, OW)].astype(jnp.float32) * (1.0 / HB)
                value = (turned[k * RB:(k + 1) * RB, :] * flips).astype(jnp.bfloat16)
                if cross:
                    side[g][0, :, pl.ds(k * OW, OW)] = value
                else:
                    out_v[pl.ds(row, RB), pl.ds((start + k) * OW, OW)] = value
            for cp in ag_from_side(g, 0) if cross else ag_from_block(g, 0):
                cp.start()

            for k in range(n):
                m = member(low + k)

                @pl.when(m != place)
                def _():
                    remote(
                        sbuf.at[m, cross], srecv.at[place, cross], a2_sem.at[0], a2_sem.at[1], peer(m)
                    ).start()

    def arrivals(g):
        return {
            0: ((1,), (2, 3), (4, 5, 6, 7)),
            1: ((0, 1), (2, 3), (4, 5, 6, 7)),
            2: ((9,), (0, 2, 1, 3), (4, 5, 6, 7)),
            4: ((9,), (10, 11), (0, 4, 1, 5, 2, 6, 3, 7)),
        }[y_weight(g)]

    def forward(level, groups):
        for g in groups:
            for slot in arrivals(g)[level]:
                ag_pass_on(g, slot)

    split = (half + 1) * (PEERS // 2)

    @pl.when(place + 1 < split)
    def _():
        pl.semaphore_wait(reply.at[0], split - 1 - place)
        owner_send(place + 1, split)

    stage_a(EARLY)
    for g in LATE:
        load(g)
        deltas(g, 1)
        if y_weight(g) == 4:
            deltas(g, 0)
        rs_start(g, 0)
        rs_start(g, 1)
    stage_b(EARLY)
    stage_c(EARLY)
    for g in LATE:
        if y_weight(g) != 4:
            deltas(g, 0)

    @pl.when(split < PEERS)
    def _():
        pl.semaphore_wait(reply.at[1], PEERS - split)
        owner_send(split, PEERS)

    stage_d(EARLY)
    stage_a(LATE)
    stage_b(LATE)
    stage_e(EARLY[:1])
    stage_c(LATE)
    stage_d(LATE)
    stage_e(EARLY[1:])
    forward(0, EARLY)
    stage_e(LATE)
    forward(1, EARLY)
    srecv[place] = sbuf[place]
    forward(0, LATE)
    forward(1, LATE)

    others = pl.ds(0, PEERS - 1)
    pltpu.make_async_copy(srecv.at[others], srecv.at[others], a2_sem.at[1]).wait()

    def finish(k, carry):
        s = pl.ds(k * 8, 8)
        sums = [srecv[k * 4 + t // 4 * 2 + t % 2, lax.rem(t // 2 % 2 + yl, 2)] for t in range(8)]
        turned = jnp.dot(jnp.concatenate(sums, axis=0), bd[...], preferred_element_type=jnp.float32)
        grad = (turned * (own * (1.0 / (HB * CUTS)))).reshape(8, RB, OW)
        mom = DECAY * mom_v[s] + grad
        mom_o[s] = mom
        master_o[s] = master_v[s] - OUTER_RATE * (grad + DECAY * mom)
        return carry

    lax.fori_loop(0, FSDP // 8, finish, 0)

    for g in range(NG):
        for slot in arrivals(g)[2]:
            ag_arrive(g, slot)
    for g in range(NG):
        for i in range(5):
            for cp in rs_copies(g, i):
                cp.wait_send()
        for i in range(y_weight(g)):
            for cp in ag_from_side(g, i):
                cp.wait_send()
        for i in range(4):
            for cp in ag_from_block(g, i):
                cp.wait_send()
    pltpu.make_async_copy(asrc.at[others], asrc.at[others], a1_send).wait()
    pltpu.make_async_copy(sbuf.at[others], sbuf.at[others], a2_sem.at[0]).wait()


def write_out(out_v, master_v, mom_v, out_hbm, master_hbm, mom_hbm, sem):
    f = lax.axis_index("fsdp")
    yl, half = lax.rem(lax.div(f, 2), 2), lax.div(f, FSDP // 2)
    copies = []
    for q in range(0, FSDP, 2):
        oz = lax.rem(q % PEERS // 2 + half * 4, 8)
        cols = pl.multiple_of(oz * 4 * OW + lax.rem(yl + q // PEERS, 2) * 2 * OW, 2 * OW)
        copies.append(pltpu.make_async_copy(
            out_v.at[:, pl.ds(q * OW, 2 * OW)], out_hbm.at[0, :, pl.ds(cols, 2 * OW)], sem.at[q // 2]
        ))
    copies += [
        pltpu.make_async_copy(master_v, master_hbm, sem.at[PEERS]),
        pltpu.make_async_copy(mom_v, mom_hbm, sem.at[PEERS + 1]),
    ]
    for cp in copies:
        cp.start()
    for cp in copies:
        cp.wait()


def step(local_params, outer_params, column_signs, delta_exponents, outer_master, outer_momentum, master_exponents):
    bf16, f32, i32 = jnp.bfloat16, jnp.float32, jnp.int32
    widths = [n * OW for _, n, _, _ in GROUPS]
    anywhere = pl.BlockSpec(memory_space=pl.ANY)
    vmem = pl.BlockSpec(memory_space=pltpu.VMEM)
    state = (FSDP, RB, OW)
    scratch = [
        pltpu.VMEM((ROWS, DIM), bf16),
        pltpu.VMEM((ROWS, DIM), bf16),
        pltpu.VMEM((1, DIM), i32),
        pltpu.VMEM((1, OW), i32),
        pltpu.VMEM((RB, DIM), bf16),
        pltpu.VMEM((DIM // HB, ROWS), i32),
        pltpu.VMEM((ROWS, DIM // HB), f32),
        pltpu.VMEM(state, f32),
        pltpu.VMEM(state, f32),
        pltpu.VMEM((RB, OW // HB, FSDP), i32),
        pltpu.VMEM((OW, HB), bf16),
        pltpu.VMEM((OW, OW), bf16),
        pltpu.VMEM((PEERS, 2, RB, OW + HB), bf16),
        pltpu.VMEM((PEERS, 2, RB, OW + HB), bf16),
        pltpu.VMEM((PEERS, 2, RB, OW), bf16),
        pltpu.VMEM((PEERS, 2, RB, OW), bf16),
    ]
    scratch += [pltpu.VMEM((2, 4, RB, w), bf16) for w in widths]
    scratch += [pltpu.VMEM((4, RB, w), bf16) for w in widths]
    scratch += [pltpu.VMEM((2, RB, w), bf16) for w in widths]
    scratch += [pltpu.VMEM((RB, w), bf16) for w in widths]
    scratch += [pltpu.VMEM((y_weight(g), RB, widths[g]), bf16) for g in LATE] * 2
    dma = pltpu.SemaphoreType.DMA
    scratch += [
        dma((PEERS, 2)), dma((6,)), dma((NG, 10)), dma((NG, 10)), dma((NG, 12)), dma((NG, 12)),
        dma, dma((PEERS,)), dma((2,)), pltpu.SemaphoreType.REGULAR((2,)),
    ]
    hbm = functools.partial(pltpu.with_memory_space_constraint, memory_space=pltpu.HBM)
    held = pl.pallas_call(
        kernel,
        out_shape=(pltpu.VMEM((ROWS, DIM), bf16), pltpu.VMEM(state, f32), pltpu.VMEM(state, f32)),
        in_specs=[anywhere] * 7,
        out_specs=(vmem,) * 3,
        scratch_shapes=scratch,
        compiler_params=pltpu.CompilerParams(
            collective_id=0, has_side_effects=True, vmem_limit_bytes=40 * 1024 * 1024
        ),
    )(
        hbm(local_params), hbm(outer_params), hbm(column_signs.reshape(1, DIM)),
        hbm(jnp.swapaxes(delta_exponents, 2, 3)), hbm(outer_master), hbm(outer_momentum),
        hbm(jnp.transpose(master_exponents, (1, 2, 0))),
    )
    return pl.pallas_call(
        write_out,
        out_shape=(
            pltpu.HBM((1, ROWS, DIM), bf16),
            pltpu.HBM(state, f32),
            pltpu.HBM(state, f32),
        ),
        in_specs=[vmem] * 3,
        out_specs=(anywhere,) * 3,
        scratch_shapes=[dma((PEERS + 2,))],
    )(*[pltpu.with_memory_space_constraint(h, pltpu.VMEM) for h in held])


def solution(mesh):
    placed = (
        P("cuts", "fsdp", None, None),
        P("fsdp", None, None),
        P(),
        P("cuts", "fsdp", None, None),
        P(None, "cuts", "fsdp"),
        P(None, "cuts", "fsdp"),
        P(None, "cuts", "fsdp"),
    )
    return jax.shard_map(
        step,
        mesh=mesh,
        in_specs=placed,
        out_specs=(P("fsdp", None, None), P(None, "cuts", "fsdp"), P(None, "cuts", "fsdp")),
        check_vma=False,
    )
```

```python
import functools
import math

import jax
import jax.numpy as jnp
from jax import lax
from jax.experimental import pallas as pl
from jax.experimental.pallas import tpu as pltpu
from jax.sharding import PartitionSpec as P

HB = 128
RB = 16
OW = 256
CUTS = 8
FSDP = 32
DIM = FSDP * OW
ROWS = CUTS * RB
LIMIT = 448.0 * math.sqrt(HB)
OUTER_RATE = 0.7
DECAY = 0.9
KEEP_MOMENTUM = OUTER_RATE * DECAY * DECAY
GRAD_IN_MASTER = OUTER_RATE * (1.0 + DECAY)
MESH = pl.DeviceIdType.MESH

XA, XB, YH = 0, 1, 2
ORDERS = ((XA, XB, YH), (XB, YH, XA), (YH, XA, XB))
SIZES = (6, 6, 4, 6, 4, 6)
PEERS = FSDP // 2


def column_groups():
    groups, start = [], 0
    for k, n in enumerate(SIZES):
        groups.append((start, n, k // 3, ORDERS[k % 3]))
        start += n
    assert start == FSDP
    return groups


GROUPS = column_groups()
NG = len(GROUPS)
EARLY, LATE = range(0, NG // 2), range(NG // 2, NG)


def y_weight(g):
    _, _, cross, order = GROUPS[g]
    return (4, 2, 1)[order.index(YH)] if cross else 0


def bits(i):
    return (i // 4, i // 2 % 2, i % 2)


def sylvester(order):
    i = lax.broadcasted_iota(jnp.int32, (order, order), 0)
    j = lax.broadcasted_iota(jnp.int32, (order, order), 1)
    t = jnp.bitwise_and(i, j)
    for s in (4, 2, 1):
        t = jnp.bitwise_xor(t, jnp.right_shift(t, s))
    return (1 - 2 * jnp.bitwise_and(t, 1)).astype(jnp.float32)


def power(exponents):
    return jnp.exp2(exponents.astype(jnp.float32)).astype(jnp.bfloat16)


def kernel(
    local_hbm, outer_hbm, signs_hbm, dexp_hbm, master_hbm, mom_hbm, mexp_hbm,
    out_v, master_o, mom_o,
    lv, ov, sv, so, flips16, dexp_v, thr, master_v, mom_v, mexp_v,
    w1, bd, asrc, abuf, sbuf, srecv,
    *rest,
):
    parts, r1, r2, r3 = (rest[k * NG:(k + 1) * NG] for k in range(4))
    rest = rest[4 * NG:]
    rx = dict(zip(LATE, rest[:len(LATE)]))
    side = dict(zip(LATE, rest[len(LATE):2 * len(LATE)]))
    ld_sem, in_sem, rs_send, rs_recv, ag_send, ag_recv, a1_send, a1_recv, a2_sem, reply = rest[2 * len(LATE):]
    c, f = lax.axis_index("cuts"), lax.axis_index("fsdp")
    x, yh = lax.div(c, 2), lax.rem(c, 2)
    z, yl, core = lax.div(f, 4), lax.rem(lax.div(f, 2), 2), lax.rem(f, 2)
    v = lax.div(x, 2)
    u = lax.rem(lax.rem(x, 2) + v, 2)
    flip_x = x + 1 - 2 * lax.rem(x, 2)
    sister = z * 4 + (1 - yl) * 2 + core
    partner = (
        (flip_x * 2 + yh, f),
        ((3 - x) * 2 + yh, f),
        (x * 2 + 1 - yh, f),
    )
    near, far = (c, sister), (x * 2 + 1 - yh, sister)
    place = z * 2 + core
    half = lax.div(place, PEERS // 2)

    def peer(m):
        return (c, lax.div(m, 2) * 4 + yl * 2 + lax.rem(m, 2))

    def member(q):
        return lax.rem(q % PEERS // 2 + half * 4, 8) * 2 + q % 2

    def line(q):
        return pl.ds(pl.multiple_of(member(q) * 2 * OW + lax.rem(yl + q // PEERS, 2) * 2 * OW, 2 * OW), 2 * OW)

    def first_row(order, flips):
        mine = [u, v, yh]
        for d, b in zip(order, flips):
            mine[d] = lax.rem(mine[d] + b, 2)
        au, av, ay = mine
        ax = av * 2 + lax.rem(au + av, 2)
        return pl.multiple_of((ax * 2 + ay) * RB, RB)

    barrier = pltpu.get_barrier_semaphore()
    for p in (*partner, near, far):
        pl.semaphore_signal(barrier, inc=1, device_id=p, device_id_type=MESH)

    small = [
        pltpu.make_async_copy(signs_hbm, sv, in_sem.at[0]),
        pltpu.make_async_copy(dexp_hbm.at[0, 0], dexp_v, in_sem.at[1]),
        pltpu.make_async_copy(master_hbm, master_v, in_sem.at[2]),
        pltpu.make_async_copy(mom_hbm, mom_v, in_sem.at[3]),
        pltpu.make_async_copy(mexp_hbm, mexp_v, in_sem.at[4]),
        pltpu.make_async_copy(signs_hbm.at[:, pl.ds(pl.multiple_of(f * OW, OW), OW)], so, in_sem.at[5]),
    ]
    loads = []
    for q in range(0, FSDP, 2):
        cols, source = pl.ds(q * OW, 2 * OW), line(q)
        loads.append((
            pltpu.make_async_copy(local_hbm.at[0, 0, :, source], lv.at[:, cols], ld_sem.at[q // 2, 0]),
            pltpu.make_async_copy(outer_hbm.at[0, :, source], ov.at[:, cols], ld_sem.at[q // 2, 1]),
        ))
    small[0].start()
    small[1].start()
    for pair in loads[:PEERS // 2]:
        for cp in pair:
            cp.start()
    for cp in small[2:]:
        cp.start()
    for pair in loads[PEERS // 2:]:
        for cp in pair:
            cp.start()

    @pl.loop(place + 1, PEERS)
    def _(m):
        pl.semaphore_signal(barrier, inc=1, device_id=peer(m), device_id_type=MESH)

    table = sylvester(HB)
    table_b = table.astype(jnp.bfloat16)
    w1[0:HB, :] = table_b
    w1[HB:OW, :] = (-table).astype(jnp.bfloat16)
    zero = jnp.zeros((HB, HB), jnp.bfloat16)
    bd[0:HB, 0:HB] = table_b
    bd[HB:OW, HB:OW] = table_b
    bd[0:HB, HB:OW] = zero
    bd[HB:OW, 0:HB] = zero

    small[0].wait()
    for q in range(0, FSDP, 2):
        row = (1 - 2 * sv[:, line(q)]).astype(jnp.float32)
        flips16[:, pl.ds(q * OW, 2 * OW)] = jnp.broadcast_to(row, (RB, 2 * OW)).astype(jnp.bfloat16)
    blocks = DIM // HB
    block = lax.broadcasted_iota(jnp.int32, (blocks, blocks), 0)
    spot = lax.broadcasted_iota(jnp.int32, (blocks, blocks), 1)
    cross = jnp.bitwise_and(jnp.right_shift(spot, 5) + yl, 1)
    wanted = jnp.bitwise_and(jnp.right_shift(spot, 2) + half * 4, 7) * 8 + cross * 4 + jnp.bitwise_and(spot, 3)
    move = jnp.where(block == wanted, 1.0, 0.0).astype(jnp.bfloat16)
    small[1].wait()
    powers = power(dexp_v[...]).astype(jnp.float32).T.astype(jnp.bfloat16)
    thr[...] = jnp.dot(powers, move, preferred_element_type=jnp.float32) * LIMIT

    def deltas(g, part):
        start, n, _, order = GROUPS[g]
        rows = [first_row(order, (part, j // 2, j % 2)) for j in range(4)]
        tiles = []
        for row in rows:
            for k in range(2 * n):
                cols = pl.ds((2 * start + k) * HB, HB)
                flips = flips16[:, cols]
                o = ov[pl.ds(row, RB), cols] * flips
                l = lv[pl.ds(row, RB), cols] * flips
                tiles.append(jnp.concatenate([o, l], axis=1))
        turned = jnp.dot(jnp.concatenate(tiles, axis=0), w1[...], preferred_element_type=jnp.float32)
        for j, row in enumerate(rows):
            limits = thr[pl.ds(row, RB), :]
            for k in range(2 * n):
                cb = 2 * start + k
                top = jnp.broadcast_to(limits[:, cb:cb + 1], (RB, HB))
                at_row = (j * 2 * n + k) * RB
                value = turned[at_row:at_row + RB, :]
                value = jnp.minimum(jnp.maximum(value, -top), top)
                parts[g][part, j, :, pl.ds(k * HB, HB)] = value.astype(jnp.bfloat16)

    def load(g):
        start, n, _, _ = GROUPS[g]
        for pair in loads[start // 2:(start + n) // 2]:
            for cp in pair:
                cp.wait()

    def remote(src, dst, send, recv, to):
        return pltpu.make_async_remote_copy(
            src_ref=src, dst_ref=dst, send_sem=send, recv_sem=recv, device_id=to, device_id_type=MESH
        )

    def kept1(g, j):
        return rx[g].at[j] if y_weight(g) == 4 else parts[g].at[0, j]

    def kept2(g, j):
        return rx[g].at[j] if y_weight(g) == 2 else kept1(g, j)

    def kept3(g):
        return rx[g].at[0] if y_weight(g) == 1 else kept2(g, 0)

    def rs_copies(g, i):
        level = (0, 0, 1, 1, 2)[i]
        order = GROUPS[g][3]
        two = pl.ds((2, 0)[i], 2) if i < 2 else None
        one = (None, None, 1, 0, None)[i]
        dst = (lambda: r1[g].at[two], lambda: r2[g].at[one], lambda: r3[g])[level]()
        sources = [
            (lambda: parts[g].at[b, two], lambda: kept1(g, 2 * b + one), lambda: kept2(g, b))[level]() for b in range(2)
        ]
        if y_weight(g) != (4, 2, 1)[level]:
            return [remote(sources[1], dst, rs_send.at[g, i], rs_recv.at[g, i], partner[order[level]])]
        other = (lambda: rx[g].at[two], lambda: rx[g].at[one], lambda: rx[g].at[0])[level]()
        return [
            remote(sources[1], dst, rs_send.at[g, i], rs_recv.at[g, i], far),
            remote(sources[0], other, rs_send.at[g, 5 + i], rs_recv.at[g, 5 + i], near),
        ]

    def rs_start(g, i):
        for cp in rs_copies(g, i):
            cp.start()

    def rs_wait(g, i):
        for cp in rs_copies(g, i):
            cp.wait_recv()

    def block_of(g, i):
        start, n, _, order = GROUPS[g]
        return out_v.at[pl.ds(first_row(order, bits(i)), RB), pl.ds(start * OW, n * OW)]

    def ag_slots(g, slot):
        return ag_send.at[g, slot], ag_recv.at[g, slot]

    def ag_from_side(g, i):
        yb, order = y_weight(g), GROUPS[g][3]
        found = []
        for w in (1, 2, 4):
            if i < w < yb:
                to = partner[order[{4: 0, 2: 1, 1: 2}[w]]]
                found.append(remote(side[g].at[i], side[g].at[i + w], *ag_slots(g, 8 + i + w), to))
        found.append(remote(side[g].at[i], block_of(g, i), *ag_slots(g, i), near))
        found.append(remote(side[g].at[i], block_of(g, i), *ag_slots(g, i + yb), far))
        return found

    def ag_from_block(g, i):
        yb, order = y_weight(g), GROUPS[g][3]
        found = []
        for w in (1, 2, 4):
            if w > i and w >= 2 * yb:
                to = partner[order[{4: 0, 2: 1, 1: 2}[w]]]
                found.append(remote(block_of(g, i), block_of(g, i), *ag_slots(g, i + w), to))
        return found

    def ag_arrive(g, slot):
        ref = side[g].at[slot - 8] if slot >= 8 else block_of(g, slot)
        remote(ref, ref, *ag_slots(g, slot), near).wait_recv()

    def ag_pass_on(g, slot):
        ag_arrive(g, slot)
        for cp in ag_from_side(g, slot - 8) if slot >= 8 else ag_from_block(g, slot):
            cp.start()

    def add(mine, other):
        return mine.astype(jnp.float32) + other.astype(jnp.float32)

    pl.semaphore_wait(barrier, 5 + place)

    @pl.loop(0, place)
    def _(m):
        other = half - lax.div(m, PEERS // 2)
        pl.semaphore_signal(reply.at[other], inc=1, device_id=peer(m), device_id_type=MESH)

    for g in EARLY:
        load(g)
        deltas(g, 1)
        rs_start(g, 0)
        rs_start(g, 1)

    for cp in small[2:]:
        cp.wait()
    own = (1 - 2 * so[...]).astype(jnp.float32)

    def prepare(k, carry):
        s = pl.ds(k * 8, 8)
        a = (master_v[s] - KEEP_MOMENTUM * mom_v[s]).reshape(8 * RB, OW) * own
        hi = a.astype(jnp.bfloat16)
        lo = (a - hi.astype(jnp.float32)).astype(jnp.bfloat16)
        turned = jnp.dot(hi, bd[...], preferred_element_type=jnp.float32)
        turned += jnp.dot(lo, bd[...], preferred_element_type=jnp.float32)
        turned = turned.astype(jnp.bfloat16)
        for t in range(8):
            to, which = k * 4 + t // 4 * 2 + t % 2, lax.rem(t // 2 % 2 + yl, 2)
            asrc[to, which, :, 0:OW] = turned[t * RB:(t + 1) * RB, :]
        return carry

    lax.fori_loop(0, FSDP // 8, prepare, 0)
    scales = [power(mexp_v[:, b, :]).astype(jnp.float32) for b in range(2)]
    first = lax.broadcasted_iota(jnp.int32, (RB, HB), 1) < HB // 2
    for s in range(FSDP):
        both = jnp.where(
            first,
            jnp.broadcast_to(scales[0][:, s:s + 1], (RB, HB)),
            jnp.broadcast_to(scales[1][:, s:s + 1], (RB, HB)),
        )
        to, which = s // 4 * 2 + s % 2, lax.rem(s // 2 % 2 + yl, 2)
        asrc[to, which, :, OW:OW + HB] = both.astype(jnp.bfloat16)

    def owner_send(low, high):
        @pl.loop(low, high)
        def _(m):
            remote(asrc.at[m], abuf.at[place], a1_send, a1_recv.at[place], peer(m)).start()

    owner_send(0, place)
    abuf[place] = asrc[place]

    for g in EARLY:
        deltas(g, 0)

    def stage_a(groups):
        for g in groups:
            rs_wait(g, 0)
            for j in (3, 2):
                kept1(g, j)[...] = add(kept1(g, j)[...], r1[g][j]).astype(jnp.bfloat16)
            if y_weight(g) != 2:
                rs_start(g, 2)
                rs_start(g, 3)

    def stage_b(groups):
        for g in groups:
            rs_wait(g, 1)
            for j in (1, 0):
                kept1(g, j)[...] = add(kept1(g, j)[...], r1[g][j]).astype(jnp.bfloat16)
            if y_weight(g) == 2:
                rs_start(g, 2)
                rs_start(g, 3)

    def stage_c(groups):
        for g in groups:
            rs_wait(g, 2)
            kept2(g, 1)[...] = add(kept2(g, 1)[...], r2[g][1]).astype(jnp.bfloat16)
            if y_weight(g) != 1:
                rs_start(g, 4)

    def stage_d(groups):
        for g in groups:
            rs_wait(g, 3)
            kept2(g, 0)[...] = add(kept2(g, 0)[...], r2[g][0]).astype(jnp.bfloat16)
            if y_weight(g) == 1:
                rs_start(g, 4)

    def stage_e(groups):
        for g in groups:
            start, n, cross, order = GROUPS[g]
            low = start % PEERS
            rs_wait(g, 4)
            if not cross:
                for k in range(n):
                    m = member(low + k)

                    @pl.when(m != place)
                    def _():
                        remote(asrc.at[m], abuf.at[m], a1_send, a1_recv.at[m], peer(m)).wait_recv()

            codes = []
            for k in range(n):
                cols = pl.ds(k * OW, OW)
                total = add(kept3(g)[:, cols], r3[g][:, cols])
                m = member(low + k)
                sbuf[m, cross] = total.astype(jnp.bfloat16)
                code = abuf[m, cross, :, 0:OW].astype(jnp.float32) - (GRAD_IN_MASTER / CUTS) * total
                scale = abuf[m, cross, :, OW:OW + HB].astype(jnp.float32) * LIMIT
                top = jnp.concatenate(
                    [jnp.broadcast_to(scale[:, b:b + 1], (RB, HB)) for b in (0, HB // 2)], axis=1
                )
                codes.append(jnp.minimum(jnp.maximum(code, -top), top).astype(jnp.bfloat16))
            turned = jnp.dot(jnp.concatenate(codes, axis=0), bd[...], preferred_element_type=jnp.float32)
            row = first_row(order, (0, 0, 0))
            for k in range(n):
                flips = flips16[:, pl.ds((low + k) * OW, OW)].astype(jnp.float32) * (1.0 / HB)
                value = (turned[k * RB:(k + 1) * RB, :] * flips).astype(jnp.bfloat16)
                if cross:
                    side[g][0, :, pl.ds(k * OW, OW)] = value
                else:
                    out_v[pl.ds(row, RB), pl.ds((start + k) * OW, OW)] = value
            for cp in ag_from_side(g, 0) if cross else ag_from_block(g, 0):
                cp.start()

            for k in range(n):
                m = member(low + k)

                @pl.when(m != place)
                def _():
                    remote(
                        sbuf.at[m, cross], srecv.at[place, cross], a2_sem.at[0], a2_sem.at[1], peer(m)
                    ).start()

    def arrivals(g):
        return {
            0: ((1,), (2, 3), (4, 5, 6, 7)),
            1: ((0, 1), (2, 3), (4, 5, 6, 7)),
            2: ((9,), (0, 2, 1, 3), (4, 5, 6, 7)),
            4: ((9,), (10, 11), (0, 4, 1, 5, 2, 6, 3, 7)),
        }[y_weight(g)]

    def forward(level, groups):
        for g in groups:
            for slot in arrivals(g)[level]:
                ag_pass_on(g, slot)

    split = (half + 1) * (PEERS // 2)

    @pl.when(place + 1 < split)
    def _():
        pl.semaphore_wait(reply.at[0], split - 1 - place)
        owner_send(place + 1, split)

    stage_a(EARLY)
    for g in LATE:
        load(g)
        deltas(g, 1)
        if y_weight(g) == 4:
            deltas(g, 0)
        rs_start(g, 0)
        rs_start(g, 1)
    stage_b(EARLY)
    stage_c(EARLY)
    for g in LATE:
        if y_weight(g) != 4:
            deltas(g, 0)

    stage_d(EARLY)

    @pl.when(split < PEERS)
    def _():
        pl.semaphore_wait(reply.at[1], PEERS - split)
        owner_send(split, PEERS)

    for g in LATE:
        stage_a([g])
        stage_b([g])
    stage_e(EARLY[:1])
    for g in LATE:
        stage_c([g])
        stage_d([g])
    stage_e(EARLY[1:])
    forward(0, EARLY)
    stage_e(LATE)
    forward(1, EARLY)
    srecv[place] = sbuf[place]
    forward(0, LATE)
    forward(1, LATE)

    others = pl.ds(0, PEERS - 1)
    pltpu.make_async_copy(srecv.at[others], srecv.at[others], a2_sem.at[1]).wait()

    def finish(k, carry):
        s = pl.ds(k * 8, 8)
        sums = [srecv[k * 4 + t // 4 * 2 + t % 2, lax.rem(t // 2 % 2 + yl, 2)] for t in range(8)]
        turned = jnp.dot(jnp.concatenate(sums, axis=0), bd[...], preferred_element_type=jnp.float32)
        grad = (turned * (own * (1.0 / (HB * CUTS)))).reshape(8, RB, OW)
        mom = DECAY * mom_v[s] + grad
        mom_o[s] = mom
        master_o[s] = master_v[s] - OUTER_RATE * (grad + DECAY * mom)
        return carry

    lax.fori_loop(0, FSDP // 8, finish, 0)

    for g in range(NG):
        for slot in arrivals(g)[2]:
            ag_arrive(g, slot)
    for g in range(NG):
        for i in range(5):
            for cp in rs_copies(g, i):
                cp.wait_send()
        for i in range(y_weight(g)):
            for cp in ag_from_side(g, i):
                cp.wait_send()
        for i in range(4):
            for cp in ag_from_block(g, i):
                cp.wait_send()
    pltpu.make_async_copy(asrc.at[others], asrc.at[others], a1_send).wait()
    pltpu.make_async_copy(sbuf.at[others], sbuf.at[others], a2_sem.at[0]).wait()


def write_out(out_v, master_v, mom_v, out_hbm, master_hbm, mom_hbm, sem):
    f = lax.axis_index("fsdp")
    yl, half = lax.rem(lax.div(f, 2), 2), lax.div(f, FSDP // 2)
    copies = []
    for q in range(0, FSDP, 2):
        oz = lax.rem(q % PEERS // 2 + half * 4, 8)
        cols = pl.multiple_of(oz * 4 * OW + lax.rem(yl + q // PEERS, 2) * 2 * OW, 2 * OW)
        copies.append(pltpu.make_async_copy(
            out_v.at[:, pl.ds(q * OW, 2 * OW)], out_hbm.at[0, :, pl.ds(cols, 2 * OW)], sem.at[q // 2]
        ))
    copies += [
        pltpu.make_async_copy(master_v, master_hbm, sem.at[PEERS]),
        pltpu.make_async_copy(mom_v, mom_hbm, sem.at[PEERS + 1]),
    ]
    for cp in copies:
        cp.start()
    for cp in copies:
        cp.wait()


def step(local_params, outer_params, column_signs, delta_exponents, outer_master, outer_momentum, master_exponents):
    bf16, f32, i32 = jnp.bfloat16, jnp.float32, jnp.int32
    widths = [n * OW for _, n, _, _ in GROUPS]
    anywhere = pl.BlockSpec(memory_space=pl.ANY)
    vmem = pl.BlockSpec(memory_space=pltpu.VMEM)
    state = (FSDP, RB, OW)
    scratch = [
        pltpu.VMEM((ROWS, DIM), bf16),
        pltpu.VMEM((ROWS, DIM), bf16),
        pltpu.VMEM((1, DIM), i32),
        pltpu.VMEM((1, OW), i32),
        pltpu.VMEM((RB, DIM), bf16),
        pltpu.VMEM((DIM // HB, ROWS), i32),
        pltpu.VMEM((ROWS, DIM // HB), f32),
        pltpu.VMEM(state, f32),
        pltpu.VMEM(state, f32),
        pltpu.VMEM((RB, OW // HB, FSDP), i32),
        pltpu.VMEM((OW, HB), bf16),
        pltpu.VMEM((OW, OW), bf16),
        pltpu.VMEM((PEERS, 2, RB, OW + HB), bf16),
        pltpu.VMEM((PEERS, 2, RB, OW + HB), bf16),
        pltpu.VMEM((PEERS, 2, RB, OW), bf16),
        pltpu.VMEM((PEERS, 2, RB, OW), bf16),
    ]
    scratch += [pltpu.VMEM((2, 4, RB, w), bf16) for w in widths]
    scratch += [pltpu.VMEM((4, RB, w), bf16) for w in widths]
    scratch += [pltpu.VMEM((2, RB, w), bf16) for w in widths]
    scratch += [pltpu.VMEM((RB, w), bf16) for w in widths]
    scratch += [pltpu.VMEM((y_weight(g), RB, widths[g]), bf16) for g in LATE] * 2
    dma = pltpu.SemaphoreType.DMA
    scratch += [
        dma((PEERS, 2)), dma((6,)), dma((NG, 10)), dma((NG, 10)), dma((NG, 12)), dma((NG, 12)),
        dma, dma((PEERS,)), dma((2,)), pltpu.SemaphoreType.REGULAR((2,)),
    ]
    hbm = functools.partial(pltpu.with_memory_space_constraint, memory_space=pltpu.HBM)
    held = pl.pallas_call(
        kernel,
        out_shape=(pltpu.VMEM((ROWS, DIM), bf16), pltpu.VMEM(state, f32), pltpu.VMEM(state, f32)),
        in_specs=[anywhere] * 7,
        out_specs=(vmem,) * 3,
        scratch_shapes=scratch,
        compiler_params=pltpu.CompilerParams(
            collective_id=0, has_side_effects=True, vmem_limit_bytes=40 * 1024 * 1024
        ),
    )(
        hbm(local_params), hbm(outer_params), hbm(column_signs.reshape(1, DIM)),
        hbm(jnp.swapaxes(delta_exponents, 2, 3)), hbm(outer_master), hbm(outer_momentum),
        hbm(jnp.transpose(master_exponents, (1, 2, 0))),
    )
    return pl.pallas_call(
        write_out,
        out_shape=(
            pltpu.HBM((1, ROWS, DIM), bf16),
            pltpu.HBM(state, f32),
            pltpu.HBM(state, f32),
        ),
        in_specs=[vmem] * 3,
        out_specs=(anywhere,) * 3,
        scratch_shapes=[dma((PEERS + 2,))],
    )(*[pltpu.with_memory_space_constraint(h, pltpu.VMEM) for h in held])


def solution(mesh):
    placed = (
        P("cuts", "fsdp", None, None),
        P("fsdp", None, None),
        P(),
        P("cuts", "fsdp", None, None),
        P(None, "cuts", "fsdp"),
        P(None, "cuts", "fsdp"),
        P(None, "cuts", "fsdp"),
    )
    return jax.shard_map(
        step,
        mesh=mesh,
        in_specs=placed,
        out_specs=(P("fsdp", None, None), P(None, "cuts", "fsdp"), P(None, "cuts", "fsdp")),
        check_vma=False,
    )
```

```python
import functools
import math

import jax
import jax.numpy as jnp
from jax import lax
from jax.experimental import pallas as pl
from jax.experimental.pallas import tpu as pltpu
from jax.sharding import PartitionSpec as P

HB = 128
RB = 16
OW = 256
CUTS = 8
FSDP = 32
DIM = FSDP * OW
ROWS = CUTS * RB
LIMIT = 448.0 * math.sqrt(HB)
OUTER_RATE = 0.7
DECAY = 0.9
KEEP_MOMENTUM = OUTER_RATE * DECAY * DECAY
GRAD_IN_MASTER = OUTER_RATE * (1.0 + DECAY)
MESH = pl.DeviceIdType.MESH

XA, XB, YH = 0, 1, 2
ORDERS = ((XA, XB, YH), (XB, YH, XA), (YH, XA, XB))
SIZES = (6, 6, 4, 6, 4, 6)
PEERS = FSDP // 2


def column_groups():
    groups, start = [], 0
    for k, n in enumerate(SIZES):
        groups.append((start, n, k // 3, ORDERS[k % 3]))
        start += n
    assert start == FSDP
    return groups


GROUPS = column_groups()
NG = len(GROUPS)
EARLY, LATE = range(0, NG // 2), range(NG // 2, NG)


def y_weight(g):
    _, _, cross, order = GROUPS[g]
    return (4, 2, 1)[order.index(YH)] if cross else 0


def bits(i):
    return (i // 4, i // 2 % 2, i % 2)


def sylvester(order):
    i = lax.broadcasted_iota(jnp.int32, (order, order), 0)
    j = lax.broadcasted_iota(jnp.int32, (order, order), 1)
    t = jnp.bitwise_and(i, j)
    for s in (4, 2, 1):
        t = jnp.bitwise_xor(t, jnp.right_shift(t, s))
    return (1 - 2 * jnp.bitwise_and(t, 1)).astype(jnp.float32)


def power(exponents):
    return jnp.exp2(exponents.astype(jnp.float32)).astype(jnp.bfloat16)


def kernel(
    local_hbm, outer_hbm, signs_hbm, dexp_hbm, master_hbm, mom_hbm, mexp_hbm,
    out_v, master_o, mom_o,
    lv, ov, sv, so, flips16, dexp_v, thr, master_v, mom_v, mexp_v,
    w1, bd, asrc, abuf, sbuf, srecv,
    *rest,
):
    parts, r1, r2, r3 = (rest[k * NG:(k + 1) * NG] for k in range(4))
    rest = rest[4 * NG:]
    rx = dict(zip(LATE, rest[:len(LATE)]))
    side = dict(zip(LATE, rest[len(LATE):2 * len(LATE)]))
    ld_sem, in_sem, rs_send, rs_recv, ag_send, ag_recv, a1_send, a1_recv, a2_sem, reply = rest[2 * len(LATE):]
    c, f = lax.axis_index("cuts"), lax.axis_index("fsdp")
    x, yh = lax.div(c, 2), lax.rem(c, 2)
    z, yl, core = lax.div(f, 4), lax.rem(lax.div(f, 2), 2), lax.rem(f, 2)
    v = lax.div(x, 2)
    u = lax.rem(lax.rem(x, 2) + v, 2)
    flip_x = x + 1 - 2 * lax.rem(x, 2)
    sister = z * 4 + (1 - yl) * 2 + core
    partner = (
        (flip_x * 2 + yh, f),
        ((3 - x) * 2 + yh, f),
        (x * 2 + 1 - yh, f),
    )
    near, far = (c, sister), (x * 2 + 1 - yh, sister)
    place = z * 2 + core
    half = lax.div(place, PEERS // 2)

    def peer(m):
        return (c, lax.div(m, 2) * 4 + yl * 2 + lax.rem(m, 2))

    def member(q):
        return lax.rem(q % PEERS // 2 + half * 4, 8) * 2 + q % 2

    def line(q):
        return pl.ds(pl.multiple_of(member(q) * 2 * OW + lax.rem(yl + q // PEERS, 2) * 2 * OW, 2 * OW), 2 * OW)

    def first_row(order, flips):
        mine = [u, v, yh]
        for d, b in zip(order, flips):
            mine[d] = lax.rem(mine[d] + b, 2)
        au, av, ay = mine
        ax = av * 2 + lax.rem(au + av, 2)
        return pl.multiple_of((ax * 2 + ay) * RB, RB)

    barrier = pltpu.get_barrier_semaphore()
    for p in (*partner, near, far):
        pl.semaphore_signal(barrier, inc=1, device_id=p, device_id_type=MESH)

    small = [
        pltpu.make_async_copy(signs_hbm, sv, in_sem.at[0]),
        pltpu.make_async_copy(dexp_hbm.at[0, 0], dexp_v, in_sem.at[1]),
        pltpu.make_async_copy(master_hbm, master_v, in_sem.at[2]),
        pltpu.make_async_copy(mom_hbm, mom_v, in_sem.at[3]),
        pltpu.make_async_copy(mexp_hbm, mexp_v, in_sem.at[4]),
        pltpu.make_async_copy(signs_hbm.at[:, pl.ds(pl.multiple_of(f * OW, OW), OW)], so, in_sem.at[5]),
    ]
    loads = []
    for q in range(0, FSDP, 2):
        cols, source = pl.ds(q * OW, 2 * OW), line(q)
        loads.append((
            pltpu.make_async_copy(local_hbm.at[0, 0, :, source], lv.at[:, cols], ld_sem.at[q // 2, 0]),
            pltpu.make_async_copy(outer_hbm.at[0, :, source], ov.at[:, cols], ld_sem.at[q // 2, 1]),
        ))
    small[0].start()
    small[1].start()
    for pair in loads[:PEERS // 2]:
        for cp in pair:
            cp.start()
    for cp in small[2:]:
        cp.start()
    for pair in loads[PEERS // 2:]:
        for cp in pair:
            cp.start()

    @pl.loop(place + 1, PEERS)
    def _(m):
        pl.semaphore_signal(barrier, inc=1, device_id=peer(m), device_id_type=MESH)

    table = sylvester(HB)
    table_b = table.astype(jnp.bfloat16)
    w1[0:HB, :] = table_b
    w1[HB:OW, :] = (-table).astype(jnp.bfloat16)
    zero = jnp.zeros((HB, HB), jnp.bfloat16)
    bd[0:HB, 0:HB] = table_b
    bd[HB:OW, HB:OW] = table_b
    bd[0:HB, HB:OW] = zero
    bd[HB:OW, 0:HB] = zero

    small[0].wait()
    for q in range(0, FSDP, 2):
        row = (1 - 2 * sv[:, line(q)]).astype(jnp.float32)
        flips16[:, pl.ds(q * OW, 2 * OW)] = jnp.broadcast_to(row, (RB, 2 * OW)).astype(jnp.bfloat16)
    blocks = DIM // HB
    block = lax.broadcasted_iota(jnp.int32, (blocks, blocks), 0)
    spot = lax.broadcasted_iota(jnp.int32, (blocks, blocks), 1)
    cross = jnp.bitwise_and(jnp.right_shift(spot, 5) + yl, 1)
    wanted = jnp.bitwise_and(jnp.right_shift(spot, 2) + half * 4, 7) * 8 + cross * 4 + jnp.bitwise_and(spot, 3)
    move = jnp.where(block == wanted, 1.0, 0.0).astype(jnp.bfloat16)
    small[1].wait()
    powers = power(dexp_v[...]).astype(jnp.float32).T.astype(jnp.bfloat16)
    thr[...] = jnp.dot(powers, move, preferred_element_type=jnp.float32) * LIMIT

    def deltas(g, part):
        start, n, _, order = GROUPS[g]
        rows = [first_row(order, (part, j // 2, j % 2)) for j in range(4)]
        tiles = []
        for row in rows:
            for k in range(2 * n):
                cols = pl.ds((2 * start + k) * HB, HB)
                flips = flips16[:, cols]
                o = ov[pl.ds(row, RB), cols] * flips
                l = lv[pl.ds(row, RB), cols] * flips
                tiles.append(jnp.concatenate([o, l], axis=1))
        turned = jnp.dot(jnp.concatenate(tiles, axis=0), w1[...], preferred_element_type=jnp.float32)
        for j, row in enumerate(rows):
            limits = thr[pl.ds(row, RB), :]
            for k in range(2 * n):
                cb = 2 * start + k
                top = jnp.broadcast_to(limits[:, cb:cb + 1], (RB, HB))
                at_row = (j * 2 * n + k) * RB
                value = turned[at_row:at_row + RB, :]
                value = jnp.minimum(jnp.maximum(value, -top), top)
                parts[g][part, j, :, pl.ds(k * HB, HB)] = value.astype(jnp.bfloat16)

    def load(g):
        start, n, _, _ = GROUPS[g]
        for pair in loads[start // 2:(start + n) // 2]:
            for cp in pair:
                cp.wait()

    def remote(src, dst, send, recv, to):
        return pltpu.make_async_remote_copy(
            src_ref=src, dst_ref=dst, send_sem=send, recv_sem=recv, device_id=to, device_id_type=MESH
        )

    def kept1(g, j):
        return rx[g].at[j] if y_weight(g) == 4 else parts[g].at[0, j]

    def kept2(g, j):
        return rx[g].at[j] if y_weight(g) == 2 else kept1(g, j)

    def kept3(g):
        return rx[g].at[0] if y_weight(g) == 1 else kept2(g, 0)

    def rs_copies(g, i):
        level = (0, 0, 1, 1, 2)[i]
        order = GROUPS[g][3]
        two = pl.ds((2, 0)[i], 2) if i < 2 else None
        one = (None, None, 1, 0, None)[i]
        dst = (lambda: r1[g].at[two], lambda: r2[g].at[one], lambda: r3[g])[level]()
        sources = [
            (lambda: parts[g].at[b, two], lambda: kept1(g, 2 * b + one), lambda: kept2(g, b))[level]() for b in range(2)
        ]
        if y_weight(g) != (4, 2, 1)[level]:
            return [remote(sources[1], dst, rs_send.at[g, i], rs_recv.at[g, i], partner[order[level]])]
        other = (lambda: rx[g].at[two], lambda: rx[g].at[one], lambda: rx[g].at[0])[level]()
        return [
            remote(sources[1], dst, rs_send.at[g, i], rs_recv.at[g, i], far),
            remote(sources[0], other, rs_send.at[g, 5 + i], rs_recv.at[g, 5 + i], near),
        ]

    def rs_start(g, i):
        for cp in rs_copies(g, i):
            cp.start()

    def rs_wait(g, i):
        for cp in rs_copies(g, i):
            cp.wait_recv()

    def block_of(g, i):
        start, n, _, order = GROUPS[g]
        return out_v.at[pl.ds(first_row(order, bits(i)), RB), pl.ds(start * OW, n * OW)]

    def ag_slots(g, slot):
        return ag_send.at[g, slot], ag_recv.at[g, slot]

    def ag_from_side(g, i):
        yb, order = y_weight(g), GROUPS[g][3]
        found = []
        for w in (1, 2, 4):
            if i < w < yb:
                to = partner[order[{4: 0, 2: 1, 1: 2}[w]]]
                found.append(remote(side[g].at[i], side[g].at[i + w], *ag_slots(g, 8 + i + w), to))
        found.append(remote(side[g].at[i], block_of(g, i), *ag_slots(g, i), near))
        found.append(remote(side[g].at[i], block_of(g, i), *ag_slots(g, i + yb), far))
        return found

    def ag_from_block(g, i):
        yb, order = y_weight(g), GROUPS[g][3]
        found = []
        for w in (1, 2, 4):
            if w > i and w >= 2 * yb:
                to = partner[order[{4: 0, 2: 1, 1: 2}[w]]]
                found.append(remote(block_of(g, i), block_of(g, i), *ag_slots(g, i + w), to))
        return found

    def ag_arrive(g, slot):
        ref = side[g].at[slot - 8] if slot >= 8 else block_of(g, slot)
        remote(ref, ref, *ag_slots(g, slot), near).wait_recv()

    def ag_pass_on(g, slot):
        ag_arrive(g, slot)
        for cp in ag_from_side(g, slot - 8) if slot >= 8 else ag_from_block(g, slot):
            cp.start()

    def add(mine, other):
        return mine.astype(jnp.float32) + other.astype(jnp.float32)

    for g in EARLY:
        load(g)
        deltas(g, 1)
        if g == 0:
            pl.semaphore_wait(barrier, 5 + place)

            @pl.loop(0, place)
            def _(m):
                other = half - lax.div(m, PEERS // 2)
                pl.semaphore_signal(reply.at[other], inc=1, device_id=peer(m), device_id_type=MESH)

        rs_start(g, 0)
        rs_start(g, 1)

    for cp in small[2:]:
        cp.wait()
    own = (1 - 2 * so[...]).astype(jnp.float32)

    def prepare(k, carry):
        s = pl.ds(k * 8, 8)
        a = (master_v[s] - KEEP_MOMENTUM * mom_v[s]).reshape(8 * RB, OW) * own
        hi = a.astype(jnp.bfloat16)
        lo = (a - hi.astype(jnp.float32)).astype(jnp.bfloat16)
        turned = jnp.dot(hi, bd[...], preferred_element_type=jnp.float32)
        turned += jnp.dot(lo, bd[...], preferred_element_type=jnp.float32)
        turned = turned.astype(jnp.bfloat16)
        for t in range(8):
            to, which = k * 4 + t // 4 * 2 + t % 2, lax.rem(t // 2 % 2 + yl, 2)
            asrc[to, which, :, 0:OW] = turned[t * RB:(t + 1) * RB, :]
        return carry

    lax.fori_loop(0, FSDP // 8, prepare, 0)
    scales = [power(mexp_v[:, b, :]).astype(jnp.float32) for b in range(2)]
    first = lax.broadcasted_iota(jnp.int32, (RB, HB), 1) < HB // 2
    for s in range(FSDP):
        both = jnp.where(
            first,
            jnp.broadcast_to(scales[0][:, s:s + 1], (RB, HB)),
            jnp.broadcast_to(scales[1][:, s:s + 1], (RB, HB)),
        )
        to, which = s // 4 * 2 + s % 2, lax.rem(s // 2 % 2 + yl, 2)
        asrc[to, which, :, OW:OW + HB] = both.astype(jnp.bfloat16)

    def owner_send(low, high):
        @pl.loop(low, high)
        def _(m):
            remote(asrc.at[m], abuf.at[place], a1_send, a1_recv.at[place], peer(m)).start()

    owner_send(0, place)
    abuf[place] = asrc[place]

    for g in EARLY:
        deltas(g, 0)

    def stage_a(groups):
        for g in groups:
            rs_wait(g, 0)
            for j in (3, 2):
                kept1(g, j)[...] = add(kept1(g, j)[...], r1[g][j]).astype(jnp.bfloat16)
            if y_weight(g) != 2:
                rs_start(g, 2)
                rs_start(g, 3)

    def stage_b(groups):
        for g in groups:
            rs_wait(g, 1)
            for j in (1, 0):
                kept1(g, j)[...] = add(kept1(g, j)[...], r1[g][j]).astype(jnp.bfloat16)
            if y_weight(g) == 2:
                rs_start(g, 2)
                rs_start(g, 3)

    def stage_c(groups):
        for g in groups:
            rs_wait(g, 2)
            kept2(g, 1)[...] = add(kept2(g, 1)[...], r2[g][1]).astype(jnp.bfloat16)
            if y_weight(g) != 1:
                rs_start(g, 4)

    def stage_d(groups):
        for g in groups:
            rs_wait(g, 3)
            kept2(g, 0)[...] = add(kept2(g, 0)[...], r2[g][0]).astype(jnp.bfloat16)
            if y_weight(g) == 1:
                rs_start(g, 4)

    def stage_e(groups):
        for g in groups:
            start, n, cross, order = GROUPS[g]
            low = start % PEERS
            rs_wait(g, 4)
            if not cross:
                for k in range(n):
                    m = member(low + k)

                    @pl.when(m != place)
                    def _():
                        remote(asrc.at[m], abuf.at[m], a1_send, a1_recv.at[m], peer(m)).wait_recv()

            codes = []
            for k in range(n):
                cols = pl.ds(k * OW, OW)
                total = add(kept3(g)[:, cols], r3[g][:, cols])
                m = member(low + k)
                sbuf[m, cross] = total.astype(jnp.bfloat16)
                code = abuf[m, cross, :, 0:OW].astype(jnp.float32) - (GRAD_IN_MASTER / CUTS) * total
                scale = abuf[m, cross, :, OW:OW + HB].astype(jnp.float32) * LIMIT
                top = jnp.concatenate(
                    [jnp.broadcast_to(scale[:, b:b + 1], (RB, HB)) for b in (0, HB // 2)], axis=1
                )
                codes.append(jnp.minimum(jnp.maximum(code, -top), top).astype(jnp.bfloat16))
            turned = jnp.dot(jnp.concatenate(codes, axis=0), bd[...], preferred_element_type=jnp.float32)
            row = first_row(order, (0, 0, 0))
            for k in range(n):
                flips = flips16[:, pl.ds((low + k) * OW, OW)].astype(jnp.float32) * (1.0 / HB)
                value = (turned[k * RB:(k + 1) * RB, :] * flips).astype(jnp.bfloat16)
                if cross:
                    side[g][0, :, pl.ds(k * OW, OW)] = value
                else:
                    out_v[pl.ds(row, RB), pl.ds((start + k) * OW, OW)] = value
            for cp in ag_from_side(g, 0) if cross else ag_from_block(g, 0):
                cp.start()

            for k in range(n):
                m = member(low + k)

                @pl.when(m != place)
                def _():
                    remote(
                        sbuf.at[m, cross], srecv.at[place, cross], a2_sem.at[0], a2_sem.at[1], peer(m)
                    ).start()

    def arrivals(g):
        return {
            0: ((1,), (2, 3), (4, 5, 6, 7)),
            1: ((0, 1), (2, 3), (4, 5, 6, 7)),
            2: ((9,), (0, 2, 1, 3), (4, 5, 6, 7)),
            4: ((9,), (10, 11), (0, 4, 1, 5, 2, 6, 3, 7)),
        }[y_weight(g)]

    def forward(level, groups):
        for g in groups:
            for slot in arrivals(g)[level]:
                ag_pass_on(g, slot)

    split = (half + 1) * (PEERS // 2)

    @pl.when(place + 1 < split)
    def _():
        pl.semaphore_wait(reply.at[0], split - 1 - place)
        owner_send(place + 1, split)

    stage_a(EARLY)
    for g in LATE:
        load(g)
        deltas(g, 1)
        if y_weight(g) == 4:
            deltas(g, 0)
        rs_start(g, 0)
        rs_start(g, 1)
    stage_b(EARLY)
    stage_c(EARLY)
    for g in LATE:
        if y_weight(g) != 4:
            deltas(g, 0)

    stage_d(EARLY)

    @pl.when(split < PEERS)
    def _():
        pl.semaphore_wait(reply.at[1], PEERS - split)
        owner_send(split, PEERS)

    for g in LATE:
        stage_a([g])
        stage_b([g])
    stage_e(EARLY[:1])
    for g in LATE:
        stage_c([g])
        stage_d([g])
    stage_e(EARLY[1:])
    forward(0, EARLY)
    stage_e(LATE)
    forward(1, EARLY)
    srecv[place] = sbuf[place]
    forward(0, LATE)
    forward(1, LATE)

    others = pl.ds(0, PEERS - 1)
    pltpu.make_async_copy(srecv.at[others], srecv.at[others], a2_sem.at[1]).wait()

    def finish(k, carry):
        s = pl.ds(k * 8, 8)
        sums = [srecv[k * 4 + t // 4 * 2 + t % 2, lax.rem(t // 2 % 2 + yl, 2)] for t in range(8)]
        turned = jnp.dot(jnp.concatenate(sums, axis=0), bd[...], preferred_element_type=jnp.float32)
        grad = (turned * (own * (1.0 / (HB * CUTS)))).reshape(8, RB, OW)
        mom = DECAY * mom_v[s] + grad
        mom_o[s] = mom
        master_o[s] = master_v[s] - OUTER_RATE * (grad + DECAY * mom)
        return carry

    lax.fori_loop(0, FSDP // 8, finish, 0)

    for g in range(NG):
        for slot in arrivals(g)[2]:
            ag_arrive(g, slot)
    for g in range(NG):
        for i in range(5):
            for cp in rs_copies(g, i):
                cp.wait_send()
        for i in range(y_weight(g)):
            for cp in ag_from_side(g, i):
                cp.wait_send()
        for i in range(4):
            for cp in ag_from_block(g, i):
                cp.wait_send()
    pltpu.make_async_copy(asrc.at[others], asrc.at[others], a1_send).wait()
    pltpu.make_async_copy(sbuf.at[others], sbuf.at[others], a2_sem.at[0]).wait()


def write_out(out_v, master_v, mom_v, out_hbm, master_hbm, mom_hbm, sem):
    f = lax.axis_index("fsdp")
    yl, half = lax.rem(lax.div(f, 2), 2), lax.div(f, FSDP // 2)
    copies = []
    for q in range(0, FSDP, 2):
        oz = lax.rem(q % PEERS // 2 + half * 4, 8)
        cols = pl.multiple_of(oz * 4 * OW + lax.rem(yl + q // PEERS, 2) * 2 * OW, 2 * OW)
        copies.append(pltpu.make_async_copy(
            out_v.at[:, pl.ds(q * OW, 2 * OW)], out_hbm.at[0, :, pl.ds(cols, 2 * OW)], sem.at[q // 2]
        ))
    copies += [
        pltpu.make_async_copy(master_v, master_hbm, sem.at[PEERS]),
        pltpu.make_async_copy(mom_v, mom_hbm, sem.at[PEERS + 1]),
    ]
    for cp in copies:
        cp.start()
    for cp in copies:
        cp.wait()


def step(local_params, outer_params, column_signs, delta_exponents, outer_master, outer_momentum, master_exponents):
    bf16, f32, i32 = jnp.bfloat16, jnp.float32, jnp.int32
    widths = [n * OW for _, n, _, _ in GROUPS]
    anywhere = pl.BlockSpec(memory_space=pl.ANY)
    vmem = pl.BlockSpec(memory_space=pltpu.VMEM)
    state = (FSDP, RB, OW)
    scratch = [
        pltpu.VMEM((ROWS, DIM), bf16),
        pltpu.VMEM((ROWS, DIM), bf16),
        pltpu.VMEM((1, DIM), i32),
        pltpu.VMEM((1, OW), i32),
        pltpu.VMEM((RB, DIM), bf16),
        pltpu.VMEM((DIM // HB, ROWS), i32),
        pltpu.VMEM((ROWS, DIM // HB), f32),
        pltpu.VMEM(state, f32),
        pltpu.VMEM(state, f32),
        pltpu.VMEM((RB, OW // HB, FSDP), i32),
        pltpu.VMEM((OW, HB), bf16),
        pltpu.VMEM((OW, OW), bf16),
        pltpu.VMEM((PEERS, 2, RB, OW + HB), bf16),
        pltpu.VMEM((PEERS, 2, RB, OW + HB), bf16),
        pltpu.VMEM((PEERS, 2, RB, OW), bf16),
        pltpu.VMEM((PEERS, 2, RB, OW), bf16),
    ]
    scratch += [pltpu.VMEM((2, 4, RB, w), bf16) for w in widths]
    scratch += [pltpu.VMEM((4, RB, w), bf16) for w in widths]
    scratch += [pltpu.VMEM((2, RB, w), bf16) for w in widths]
    scratch += [pltpu.VMEM((RB, w), bf16) for w in widths]
    scratch += [pltpu.VMEM((y_weight(g), RB, widths[g]), bf16) for g in LATE] * 2
    dma = pltpu.SemaphoreType.DMA
    scratch += [
        dma((PEERS, 2)), dma((6,)), dma((NG, 10)), dma((NG, 10)), dma((NG, 12)), dma((NG, 12)),
        dma, dma((PEERS,)), dma((2,)), pltpu.SemaphoreType.REGULAR((2,)),
    ]
    hbm = functools.partial(pltpu.with_memory_space_constraint, memory_space=pltpu.HBM)
    held = pl.pallas_call(
        kernel,
        out_shape=(pltpu.VMEM((ROWS, DIM), bf16), pltpu.VMEM(state, f32), pltpu.VMEM(state, f32)),
        in_specs=[anywhere] * 7,
        out_specs=(vmem,) * 3,
        scratch_shapes=scratch,
        compiler_params=pltpu.CompilerParams(
            collective_id=0, has_side_effects=True, vmem_limit_bytes=40 * 1024 * 1024
        ),
    )(
        hbm(local_params), hbm(outer_params), hbm(column_signs.reshape(1, DIM)),
        hbm(jnp.swapaxes(delta_exponents, 2, 3)), hbm(outer_master), hbm(outer_momentum),
        hbm(jnp.transpose(master_exponents, (1, 2, 0))),
    )
    return pl.pallas_call(
        write_out,
        out_shape=(
            pltpu.HBM((1, ROWS, DIM), bf16),
            pltpu.HBM(state, f32),
            pltpu.HBM(state, f32),
        ),
        in_specs=[vmem] * 3,
        out_specs=(anywhere,) * 3,
        scratch_shapes=[dma((PEERS + 2,))],
    )(*[pltpu.with_memory_space_constraint(h, pltpu.VMEM) for h in held])


def solution(mesh):
    placed = (
        P("cuts", "fsdp", None, None),
        P("fsdp", None, None),
        P(),
        P("cuts", "fsdp", None, None),
        P(None, "cuts", "fsdp"),
        P(None, "cuts", "fsdp"),
        P(None, "cuts", "fsdp"),
    )
    return jax.shard_map(
        step,
        mesh=mesh,
        in_specs=placed,
        out_specs=(P("fsdp", None, None), P(None, "cuts", "fsdp"), P(None, "cuts", "fsdp")),
        check_vma=False,
    )
```
